512 devices in a mesh: ctx: 32 (over x_lo, y, core), nar: 16 (over x_hi, z).
Axes of the slice: x: 4 (x_hi: 2, x_lo: 2; x = x_hi * 2 + x_lo), y: 8, z: 8, core: 2. Of those that a mesh axis runs over, the one named last changes fastest.
Arguments:
- q_proj: bfloat16 [64, 262144], P(None, ('ctx', 'nar')), may hold values from -6 to 6
- k_proj: bfloat16 [64, 262144], P(None, ('ctx', 'nar')), may hold values from -6 to 6
- v_proj: bfloat16 [64, 262144], P(None, ('ctx', 'nar')), may hold values from -6 to 6
- skip_gain: float32 [64], replicated, may hold values from -1 to 1
- spectrum: float32 [2, 2, 64, 262144], P(None, None, None, ('ctx', 'nar')), may hold values from -6 to 6
Outputs:
- gated_output: bfloat16 [64, 262144], P(None, ('ctx', 'nar'))
The draws below stay inside these ranges and needn't reach their ends.
All inputs are finite; a program needn't handle non-finite values.
Results may differ from the reference program's by a relative error of at most 0.0025.
Values sent between devices are 32-bit elements; how exact they have to be, the bound alone decides.
No kernel may reach another device: no remote copies, remote signals or barrier semaphores. Data moves between devices by JAX's collectives and lax.ppermute only.
A program may use at most 64 MiB of HBM per device.

```python
import jax
import jax.numpy as jnp
import numpy as np
from jax import lax

CH = 64
T_DEV = 512
LENGTH = 262144
N_CTX = 32
N_NAR = 16


def shard_levels(rng, extent, cuts, smallest, top_value):
    factor_of = 1.0
    for position, shards_of in cuts:
        draws = jax.random.uniform(jax.random.fold_in(jax.random.fold_in(rng, 6), position), (shards_of,), jnp.float32, smallest / len(cuts), top_value / len(cuts))
        factor_of = factor_of * jnp.repeat(jnp.exp(draws), extent[position] // shards_of).reshape((-1,) + (1,) * (len(extent) - 1 - position))
    return factor_of


def centred(stream_key, shape, width, limit, pieces=(), kind=jnp.bfloat16):
    result = width * jax.random.normal(stream_key, shape, jnp.float32)
    if pieces:
        result = result * shard_levels(stream_key, shape, pieces, -0.22, 0.18)
    return jnp.clip(result, -limit, limit).astype(kind)


def setup_inputs(seed: int = 0) -> dict:
    streams_of = jax.random.split(jax.random.key(seed), 6)
    return {
        "q_proj": centred(streams_of[0], (CH, LENGTH), 1.0, 6.0, ((1, 512),)),
        "k_proj": centred(streams_of[1], (CH, LENGTH), 1.0, 6.0, ((1, 512),)),
        "v_proj": centred(streams_of[2], (CH, LENGTH), 1.0, 6.0, ((1, 512),)),
        "skip_gain": jnp.clip(jax.random.uniform(streams_of[3], (CH,), jnp.float32, -1.0, 1.0), -1.0, 1.0),
        "spectrum": centred(streams_of[4], (2, 2, CH, LENGTH), 1.0, 6.0, ((3, 512),), jnp.float32),
    }


def reversed_order(count):
    bit_count = count.bit_length() - 1
    flipped_list = []
    for number in range(count):
        flipped = 0
        for bit_place in range(bit_count):
            flipped = flipped | (((number >> bit_place) & 1) << (bit_count - 1 - bit_place))
        flipped_list.append(flipped)
    return np.array(flipped_list, dtype=np.int32)


def reference(q_proj, k_proj, v_proj, skip_gain, spectrum):
    length = T_DEV * N_CTX * N_NAR
    product = k_proj.astype(jnp.float32) * v_proj.astype(jnp.float32)
    layout = spectrum.reshape(2, 2, CH, N_CTX, N_NAR, T_DEV)
    layout = layout[:, :, :, reversed_order(N_CTX)]
    natural = jnp.transpose(layout, (0, 1, 2, 5, 4, 3)).reshape(2, 2, CH, length)
    merged = jnp.stack([natural[0], natural[1]], axis=-1).reshape(2, CH, 2 * length)
    filters = lax.complex(merged[0], merged[1])

    def convolve(operands):
        signal, response = operands
        padded = jnp.concatenate([signal, jnp.zeros_like(signal)])
        return jnp.real(jnp.fft.ifft(jnp.fft.fft(padded) * response))[:length]

    convolved = lax.map(convolve, (product, filters))
    gated = q_proj.astype(jnp.float32) * (convolved + skip_gain[:, None] * product)
    return gated.astype(jnp.bfloat16)
```

```python
import math

import jax
import jax.numpy as jnp
import ml_dtypes
import numpy as np
from jax import lax
from jax.experimental import pallas as pl
from jax.experimental.pallas import tpu as pltpu
from jax.sharding import PartitionSpec as P

G = 32
H = 16
T = 512
LANES = 128
CHUNKS = T // LANES
ROWS = 2 * CHUNKS
FULL = 2 * G * H * T
VMEM_LIMIT = 24 * 1024 * 1024


def bit_reverse(value, bits):
    out = 0
    for place in range(bits):
        out |= (value >> place & 1) << (bits - 1 - place)
    return out


def block_freqs(j):
    first = [0, 32] if j == 0 else [j, 64 - j]
    return first + [16 + j, 48 - j]


def add(a, b):
    if a is None:
        return b
    return a if b is None else a + b


def sub(a, b):
    if b is None:
        return a
    return -b if a is None else a - b


def twist(value, steps, period):
    re, im = value
    eighth = 8 * steps % (8 * period)
    if eighth == 0:
        return value
    if eighth == 2 * period:
        return -im, re
    if eighth == 4 * period:
        return -re, -im
    if eighth == 6 * period:
        return im, -re
    c = math.cos(2 * math.pi * steps / period)
    s = math.sin(2 * math.pi * steps / period)
    if abs(abs(c) - abs(s)) < 1e-12:
        r = math.sqrt(0.5)
        cs, ss = math.copysign(1.0, c), math.copysign(1.0, s)
        a = re if cs > 0 else -re
        b = im if cs > 0 else -im
        return (
            ((a - im) if ss > 0 else (a + im)) * r,
            ((b + re) if ss > 0 else (b - re)) * r,
        )
    return re * c - im * s, re * s + im * c


def real_forward(x):
    n = len(x)
    if n == 2:
        return [(add(x[0], x[1]), None), (sub(x[0], x[1]), None)]
    even, odd = real_forward(x[0::2]), real_forward(x[1::2])
    out = [None] * (n // 2 + 1)
    out[0] = (even[0][0] + odd[0][0], None)
    out[n // 2] = (even[0][0] - odd[0][0], None)
    out[n // 4] = (even[n // 4][0], -odd[n // 4][0])
    for k in range(1, n // 4):
        tr, ti = twist(odd[k], -k, n)
        er, ei = even[k]
        out[k] = (er + tr, ei + ti)
        out[n // 2 - k] = (er - tr, ti - ei)
    return out


def real_inverse(x):
    n = 2 * (len(x) - 1)
    if n == 2:
        return [x[0][0] + x[1][0]]
    even, odd = [None] * (n // 4 + 1), [None] * (n // 4 + 1)
    even[0] = (x[0][0] + x[n // 2][0], None)
    odd[0] = (x[0][0] - x[n // 2][0], None)
    even[n // 4] = (2.0 * x[n // 4][0], None)
    odd[n // 4] = (-2.0 * x[n // 4][1], None)
    for k in range(1, n // 4):
        ar, ai = x[k]
        br, bi = x[n // 2 - k]
        even[k] = (ar + br, ai - bi)
        odd[k] = twist((ar - br, ai + bi), k, n)
    out = [None] * (n // 2)
    out[0::2], out[1::2] = real_inverse(even), real_inverse(odd)
    return out


def complex_transform(x, sign):
    n = len(x)
    if n == 1:
        return x
    even, odd = complex_transform(x[0::2], sign), complex_transform(x[1::2], sign)
    low, high = [], []
    for k in range(n // 2):
        tr, ti = twist(odd[k], sign * k, n)
        er, ei = even[k]
        low.append((er + tr, ei + ti))
        high.append((er - tr, ei - ti))
    return low + high


def times(a, b):
    return a[0] * b[0] - a[1] * b[1], a[0] * b[1] + a[1] * b[0]


def times_conj(a, b):
    return a[0] * b[0] + a[1] * b[1], a[1] * b[0] - a[0] * b[1]


SEND_A = 5 * ROWS
SEND_B = 12 * ROWS
SEND_C = 4 * ROWS


def pack_kernel(k_ref, v_ref, spec_ref, out_ref):
    product = k_ref[...].astype(jnp.float32) * v_ref[...].astype(jnp.float32)
    for half in range(2):
        rows = slice(half * G, half * G + G)
        for chunk in range(CHUNKS):
            cols = slice(chunk * LANES, (chunk + 1) * LANES)
            place = half * CHUNKS + chunk
            out_ref[pl.ds(place, G, stride=SEND_A), :] = product[rows, cols]
            for part in range(4):
                out_ref[pl.ds((part + 1) * ROWS + place, G, stride=SEND_A), :] = spec_ref[
                    part, rows, cols
                ]


def coarse_kernel(in_ref, out_ref):
    tokens = [in_ref[pl.ds(g * SEND_A, ROWS), :] for g in range(G)]
    freqs = real_forward(tokens + [None] * G)
    items = [(freqs[0][0], freqs[32][0])] + freqs[1:32]
    for j in range(H):
        base = j * SEND_B
        for e in range(2):
            for part in range(2):
                out_ref[pl.ds(base + (2 * e + part) * ROWS, ROWS), :] = items[j + 16 * e][part]
        for slot, q in enumerate(block_freqs(j)):
            source = bit_reverse(q >> 1, 5) * SEND_A + (1 + 2 * (q & 1)) * ROWS
            out_ref[pl.ds(base + (4 + 2 * slot) * ROWS, 2 * ROWS), :] = in_ref[
                pl.ds(source, 2 * ROWS), :
            ]


def split(value):
    high = value.astype(jnp.bfloat16)
    return high, (value - high.astype(jnp.float32)).astype(jnp.bfloat16)


def dense(high_ref, low_ref, table_high, table_low):
    def dot(a, b):
        return jnp.dot(a[...], b[...], preferred_element_type=jnp.float32)

    return dot(high_ref, table_high) + (dot(low_ref, table_high) + dot(high_ref, table_low))


def filter_kernel(
    j_ref, step_ref, in_ref, slow_ref, fast_ref, high_ref, low_ref, out_ref,
    re_ref, im_ref, turn_ref, xh_ref, xl_ref,
):
    j = j_ref[0]
    packed = j == 0
    for e in range(2):
        pairs = [[], []]
        for h in range(H):
            re = in_ref[pl.ds(h * SEND_B + 2 * e * ROWS, ROWS), :]
            im = in_ref[pl.ds(h * SEND_B + (2 * e + 1) * ROWS, ROWS), :]
            if e == 0:
                zero = jnp.zeros_like(im)
                pairs[0].append((re, jnp.where(packed, zero, im)))
                pairs[1].append((jnp.where(packed, im, re), jnp.where(packed, zero, -im)))
            else:
                pairs[0].append((re, im))
                pairs[1].append((re, -im))
        for side in range(2):
            slot = 2 * e + side
            turned = []
            for h in range(H):
                at = ((j * 4 + slot) * H + h) * 2
                turned.append(times(pairs[side][h], (step_ref[at], step_ref[at + 1])))
            slow = (slow_ref[j, slot, 0], slow_ref[j, slot, 1])
            for kh, value in enumerate(complex_transform(turned, -1)):
                turn = times(slow, (fast_ref[kh, 0], fast_ref[kh, 1]))
                at = slot * H + kh
                turn_ref[at, 0], turn_ref[at, 1] = turn
                re_ref[pl.ds(at * ROWS, ROWS), :], im_ref[pl.ds(at * ROWS, ROWS), :] = times(
                    value, turn
                )
    half_rows = 4 * 2 * H
    for block in range(8):
        slot, ch = block // 2, block % 2
        for part, ref in enumerate((re_ref, im_ref)):
            rows = slice(part * half_rows + block * H, part * half_rows + (block + 1) * H)
            for chunk in range(CHUNKS):
                cols = slice(chunk * LANES, (chunk + 1) * LANES)
                start = slot * H * ROWS + ch * CHUNKS + chunk
                high, low = split(ref[pl.ds(start, H, stride=ROWS), :])
                xh_ref[rows, cols] = high
                xl_ref[rows, cols] = low
    mixed = dense(xh_ref, xl_ref, high_ref, low_ref)
    for block in range(8):
        slot, ch = block // 2, block % 2
        top = slice(block * H, (block + 1) * H)
        bottom = slice(half_rows + block * H, half_rows + (block + 1) * H)
        for chunk in range(CHUNKS):
            cols = slice(chunk * LANES, (chunk + 1) * LANES)
            sine_cols = slice(T + chunk * LANES, T + (chunk + 1) * LANES)
            value = (
                mixed[top, cols] + mixed[bottom, sine_cols],
                mixed[bottom, cols] - mixed[top, sine_cols],
            )
            start = (4 + 2 * slot) * ROWS + ch * CHUNKS + chunk
            response = (
                in_ref[pl.ds(start, H, stride=SEND_B), :],
                in_ref[pl.ds(start + ROWS, H, stride=SEND_B), :],
            )
            filtered = times(value, response)
            for rows, part in ((top, 0), (bottom, 1)):
                high, low = split(filtered[part])
                xh_ref[rows, cols] = high
                xl_ref[rows, cols] = low
    mixed = dense(xh_ref, xl_ref, high_ref, low_ref)
    for block in range(8):
        slot, ch = block // 2, block % 2
        top = slice(block * H, (block + 1) * H)
        bottom = slice(half_rows + block * H, half_rows + (block + 1) * H)
        for chunk in range(CHUNKS):
            cols = slice(chunk * LANES, (chunk + 1) * LANES)
            sine_cols = slice(T + chunk * LANES, T + (chunk + 1) * LANES)
            start = slot * H * ROWS + ch * CHUNKS + chunk
            re_ref[pl.ds(start, H, stride=ROWS), :] = mixed[top, cols] - mixed[bottom, sine_cols]
            im_ref[pl.ds(start, H, stride=ROWS), :] = mixed[bottom, cols] + mixed[top, sine_cols]
    for e in range(2):
        sides = []
        for side in range(2):
            slot = 2 * e + side
            values = []
            for kh in range(H):
                at = slot * H + kh
                value = (re_ref[pl.ds(at * ROWS, ROWS), :], im_ref[pl.ds(at * ROWS, ROWS), :])
                values.append(times_conj(value, (turn_ref[at, 0], turn_ref[at, 1])))
            values = complex_transform(values, 1)
            for h in range(H):
                at = ((j * 4 + slot) * H + h) * 2
                values[h] = times_conj(values[h], (step_ref[at], step_ref[at + 1]))
            sides.append(values)
        for h in range(H):
            (ar, ai), (br, bi) = sides[0][h], sides[1][h]
            re, im = (ar + br) * (0.5 / FULL), (ai - bi) * (0.5 / FULL)
            if e == 0:
                re = jnp.where(packed, ar * (1.0 / FULL), re)
                im = jnp.where(packed, br * (1.0 / FULL), im)
            out_ref[pl.ds(h * SEND_C + 2 * e * ROWS, ROWS), :] = re
            out_ref[pl.ds(h * SEND_C + (2 * e + 1) * ROWS, ROWS), :] = im


def uncoarse_kernel(in_ref, out_ref):
    def item(i):
        base = i % 16 * SEND_C + i // 16 * 2 * ROWS
        return in_ref[pl.ds(base, ROWS), :], in_ref[pl.ds(base + ROWS, ROWS), :]

    first = item(0)
    freqs = [(first[0], None)] + [item(i) for i in range(1, 32)] + [(first[1], None)]
    for g, value in enumerate(real_inverse(freqs)):
        out_ref[pl.ds(g * ROWS, ROWS), :] = value


def gate_kernel(in_ref, q_ref, k_ref, v_ref, gain_ref, out_ref):
    channels = q_ref.shape[0]
    row = lax.broadcasted_iota(jnp.int32, (channels, channels), 0)
    col = lax.broadcasted_iota(jnp.int32, (channels, channels), 1)
    spread = jnp.broadcast_to(gain_ref[...], (channels, channels))
    gain = jnp.sum(jnp.where(row == col, spread, 0.0), axis=1, keepdims=True)
    product = k_ref[...].astype(jnp.float32) * v_ref[...].astype(jnp.float32)
    convolved = jnp.concatenate(
        [
            jnp.concatenate(
                [
                    in_ref[pl.ds(half * CHUNKS + chunk, G, stride=ROWS), :]
                    for chunk in range(CHUNKS)
                ],
                axis=1,
            )
            for half in range(2)
        ],
        axis=0,
    )
    gated = q_ref[...].astype(jnp.float32) * (convolved + gain * product)
    out_ref[...] = gated.astype(jnp.bfloat16)


def split_table(table):
    high = table.astype(np.float32).astype(ml_dtypes.bfloat16)
    low = (table - high.astype(np.float64)).astype(np.float32).astype(ml_dtypes.bfloat16)
    return high, low


def tables():
    t = np.arange(T)
    angle = 2 * np.pi * (t[:, None] * t[None, :] % T) / T
    high, low = split_table(np.concatenate([np.cos(angle), np.sin(angle)], axis=1))
    freqs = np.array([block_freqs(j) for j in range(H)])
    step = 2 * np.pi * (freqs[:, :, None] * np.arange(H) % (2 * G * H)) / (2 * G * H)
    step = np.stack([np.cos(step), -np.sin(step)], axis=-1).reshape(-1).astype(np.float32)

    def rows_of(angles):
        pair = np.stack([np.cos(angles), -np.sin(angles)], axis=-2)
        pair = pair.reshape(pair.shape[:-1] + (CHUNKS, LANES))
        return np.concatenate([pair, pair], axis=-2).astype(np.float32)

    slow = rows_of(2 * np.pi * (freqs[:, :, None] * t % FULL) / FULL)
    fast = rows_of(2 * np.pi * (np.arange(H)[:, None] * t % (H * T)) / (H * T))
    return high, low, step, slow, fast


def call(kernel, shape, in_specs=None, dtype=jnp.float32, scratch=()):
    extra = {} if in_specs is None else {"in_specs": in_specs}
    return pl.pallas_call(
        kernel,
        out_shape=jax.ShapeDtypeStruct(shape, dtype),
        scratch_shapes=list(scratch),
        compiler_params=pltpu.CompilerParams(vmem_limit_bytes=VMEM_LIMIT),
        **extra,
    )


def exchange(value, axis, count):
    blocks = value.reshape(count, -1, LANES)
    return lax.all_to_all(blocks, axis, 0, 0, tiled=True).reshape(-1, LANES)


VMEM = pl.BlockSpec(memory_space=pltpu.VMEM)
SMEM = pl.BlockSpec(memory_space=pltpu.SMEM)


def run_filter(position, value):
    high, low, step, slow, fast = tables()
    rows = 4 * H * ROWS
    return call(
        filter_kernel,
        (H * SEND_C, LANES),
        in_specs=[SMEM, SMEM] + [VMEM] * 5,
        scratch=[
            pltpu.VMEM((rows, LANES), jnp.float32),
            pltpu.VMEM((rows, LANES), jnp.float32),
            pltpu.VMEM((4 * H, 2, ROWS, LANES), jnp.float32),
            pltpu.VMEM((16 * H, T), jnp.bfloat16),
            pltpu.VMEM((16 * H, T), jnp.bfloat16),
        ],
    )(position, step, value, slow, fast, high, low)


def local(q_proj, k_proj, v_proj, skip_gain, spectrum):
    channels, tokens = q_proj.shape
    value = call(pack_kernel, (G * SEND_A, LANES))(
        k_proj, v_proj, spectrum.reshape(4, channels, tokens)
    )
    value = exchange(value, "ctx", G)
    value = call(coarse_kernel, (H * SEND_B, LANES))(value)
    value = exchange(value, "nar", H)
    value = run_filter(lax.axis_index("nar").astype(jnp.int32).reshape(1), value)
    value = exchange(value, "nar", H)
    value = call(uncoarse_kernel, (G * ROWS, LANES))(value)
    value = exchange(value, "ctx", G)
    return call(gate_kernel, (channels, tokens), dtype=jnp.bfloat16)(
        value, q_proj, k_proj, v_proj, skip_gain.reshape(1, channels)
    )


def solution(mesh):
    placed = (
        P(None, ("ctx", "nar")),
        P(None, ("ctx", "nar")),
        P(None, ("ctx", "nar")),
        P(),
        P(None, None, None, ("ctx", "nar")),
    )
    return jax.shard_map(
        local, mesh=mesh, in_specs=placed, out_specs=P(None, ("ctx", "nar")), check_vma=False
    )
```

```python
import math

import jax
import jax.numpy as jnp
import ml_dtypes
import numpy as np
from jax import lax
from jax.experimental import pallas as pl
from jax.experimental.pallas import tpu as pltpu
from jax.sharding import Mesh, PartitionSpec as P

AXES = ("xl", "yh", "yl", "core", "xh", "zh", "zl")
SIZES = (2, 4, 2, 2, 2, 4, 2)
FAR = ("xl", "yh", "zh")
NEAR = ("yl", "core", "xh", "zl")
A = 8
ZH = 4
N_FAR = A * ZH
N_NEAR = 16
D = 64
T = 512
LANES = 128
CHUNKS = T // LANES
ROWS = 2 * CHUNKS
FULL = 2 * A * D * T
VMEM_LIMIT = 24 * 1024 * 1024


def item_freqs(i):
    return (0, 8) if i == 0 else (i, 16 - i)


def source_of(q):
    xl, y2, y1 = q >> 1 & 1, q >> 2 & 1, q >> 3 & 1
    return q & 1, xl * 4 + y2 * 2 + y1


def digit(w, zh):
    return (w >> 1) * 8 + zh * 2 + (w & 1)


def freq_place(kd):
    y0, core, z0, z1, z2, xh = (kd >> bit & 1 for bit in range(6))
    return y0 * 8 + core * 4 + xh * 2 + z0, z2 * 2 + z1


def add(a, b):
    if a is None:
        return b
    return a if b is None else a + b


def sub(a, b):
    if b is None:
        return a
    return -b if a is None else a - b


def twist(value, steps, period):
    re, im = value
    eighth = 8 * steps % (8 * period)
    if eighth == 0:
        return value
    if eighth == 2 * period:
        return -im, re
    if eighth == 4 * period:
        return -re, -im
    if eighth == 6 * period:
        return im, -re
    c = math.cos(2 * math.pi * steps / period)
    s = math.sin(2 * math.pi * steps / period)
    if abs(abs(c) - abs(s)) < 1e-12:
        r = math.sqrt(0.5)
        cs, ss = math.copysign(1.0, c), math.copysign(1.0, s)
        a = re if cs > 0 else -re
        b = im if cs > 0 else -im
        return (
            ((a - im) if ss > 0 else (a + im)) * r,
            ((b + re) if ss > 0 else (b - re)) * r,
        )
    return re * c - im * s, re * s + im * c


def real_forward(x):
    n = len(x)
    if n == 2:
        return [(add(x[0], x[1]), None), (sub(x[0], x[1]), None)]
    even, odd = real_forward(x[0::2]), real_forward(x[1::2])
    out = [None] * (n // 2 + 1)
    out[0] = (even[0][0] + odd[0][0], None)
    out[n // 2] = (even[0][0] - odd[0][0], None)
    out[n // 4] = (even[n // 4][0], -odd[n // 4][0])
    for k in range(1, n // 4):
        tr, ti = twist(odd[k], -k, n)
        er, ei = even[k]
        out[k] = (er + tr, ei + ti)
        out[n // 2 - k] = (er - tr, ti - ei)
    return out


def real_inverse(x):
    n = 2 * (len(x) - 1)
    if n == 2:
        return [x[0][0] + x[1][0]]
    even, odd = [None] * (n // 4 + 1), [None] * (n // 4 + 1)
    even[0] = (x[0][0] + x[n // 2][0], None)
    odd[0] = (x[0][0] - x[n // 2][0], None)
    even[n // 4] = (2.0 * x[n // 4][0], None)
    odd[n // 4] = (-2.0 * x[n // 4][1], None)
    for k in range(1, n // 4):
        ar, ai = x[k]
        br, bi = x[n // 2 - k]
        even[k] = (ar + br, ai - bi)
        odd[k] = twist((ar - br, ai + bi), k, n)
    out = [None] * (n // 2)
    out[0::2], out[1::2] = real_inverse(even), real_inverse(odd)
    return out


def complex_transform(x, sign):
    n = len(x)
    if n == 1:
        return x
    even, odd = complex_transform(x[0::2], sign), complex_transform(x[1::2], sign)
    low, high = [], []
    for k in range(n // 2):
        tr, ti = twist(odd[k], sign * k, n)
        er, ei = even[k]
        low.append((er + tr, ei + ti))
        high.append((er - tr, ei - ti))
    return low + high


def times(a, b):
    return a[0] * b[0] - a[1] * b[1], a[0] * b[1] + a[1] * b[0]


def times_conj(a, b):
    return a[0] * b[0] + a[1] * b[1], a[1] * b[0] - a[0] * b[1]


SEND_A = 5 * ROWS
SEND_B = 12 * ROWS
SEND_C = 4 * ROWS


def pack_kernel(k_hbm, v_hbm, spec_hbm, out_ref, k_ref, v_ref, spec_ref, sems):
    copies = [
        pltpu.make_async_copy(source, target, sems.at[i])
        for i, (source, target) in enumerate(
            ((k_hbm, k_ref), (v_hbm, v_ref), (spec_hbm, spec_ref))
        )
    ]
    for copy in copies:
        copy.start()
    copies[0].wait()
    copies[1].wait()
    product = k_ref[...].astype(jnp.float32) * v_ref[...].astype(jnp.float32)
    for half in range(2):
        rows = slice(half * N_FAR, (half + 1) * N_FAR)
        for chunk in range(CHUNKS):
            cols = slice(chunk * LANES, (chunk + 1) * LANES)
            place = half * CHUNKS + chunk
            out_ref[pl.ds(place, N_FAR, stride=SEND_A), :] = product[rows, cols]
    copies[2].wait()
    for half in range(2):
        rows = slice(half * N_FAR, (half + 1) * N_FAR)
        for chunk in range(CHUNKS):
            cols = slice(chunk * LANES, (chunk + 1) * LANES)
            for parity in range(2):
                for part in range(2):
                    place = (1 + 2 * parity + half) * ROWS + part * CHUNKS + chunk
                    out_ref[pl.ds(place, N_FAR, stride=SEND_A), :] = spec_ref[
                        2 * parity + part, rows, cols
                    ]


def upper_rows():
    return lax.broadcasted_iota(jnp.int32, (ROWS, LANES), 0) < CHUNKS


def swap_halves(value):
    return pltpu.roll(value, CHUNKS, 0)


def regroup(first, second, upper):
    return (
        jnp.where(upper, first, swap_halves(second)),
        jnp.where(upper, swap_halves(first), second),
    )


def coarse_kernel(in_ref, out_ref):
    upper = upper_rows()
    for zh in range(ZH):
        tokens = [in_ref[pl.ds((a * ZH + zh) * SEND_A, ROWS), :] for a in range(A)]
        freqs = real_forward(tokens + [None] * A)
        items = [(freqs[0][0], freqs[A][0])] + freqs[1:A]
        for i in range(A):
            for ch, value in enumerate(regroup(items[i][0], items[i][1], upper)):
                base = (2 * i + ch) * SEND_B
                out_ref[pl.ds(base + zh * ROWS, ROWS), :] = value
                for side, q in enumerate(item_freqs(i)):
                    parity, a = source_of(q)
                    source = (a * ZH + zh) * SEND_A + (1 + 2 * parity + ch) * ROWS
                    target = base + (ZH + side * ZH + zh) * ROWS
                    out_ref[pl.ds(target, ROWS), :] = in_ref[pl.ds(source, ROWS), :]


def split(value):
    high = value.astype(jnp.bfloat16)
    return high, (value - high.astype(jnp.float32)).astype(jnp.bfloat16)


def dense(high_ref, low_ref, table_high, table_low):
    def dot(a, b):
        return jnp.dot(a[...], b[...], preferred_element_type=jnp.float32)

    return dot(high_ref, table_high) + (dot(low_ref, table_high) + dot(high_ref, table_low))


def filter_kernel(
    i_ref, in_ref, slow_ref, fast_ref, high_ref, low_ref, out_ref, re_ref, im_ref, xh_ref, xl_ref
):
    item = i_ref[0]
    packed = item == 0
    upper = upper_rows()
    keep = jnp.logical_or(upper, packed)
    signs = jnp.where(upper, 1.0, -1.0) * jnp.where(packed, 0.0, 1.0)
    values = [None] * D
    for w in range(N_NEAR):
        for zh in range(ZH):
            d = digit(w, zh)
            value = in_ref[pl.ds(w * SEND_B + zh * ROWS, ROWS), :]
            other = swap_halves(value)
            pair = (jnp.where(keep, value, other), jnp.where(upper, other, value) * signs)
            values[d] = times(pair, (slow_ref[item, d, 0], slow_ref[item, d, 1]))
    for kd, value in enumerate(complex_transform(values, -1)):
        w, zh = freq_place(kd)
        at = (zh * N_NEAR + w) * ROWS
        re_ref[pl.ds(at, ROWS), :], im_ref[pl.ds(at, ROWS), :] = times(
            value, (fast_ref[kd, 0], fast_ref[kd, 1])
        )
    half_rows = 2 * D
    blocks = []
    for side in range(2):
        for zh in range(ZH):
            first = (side * ZH + zh) * N_NEAR
            blocks.append(
                (
                    slice(first, first + N_NEAR),
                    slice(half_rows + first, half_rows + first + N_NEAR),
                    zh * N_NEAR * ROWS + side * CHUNKS,
                    (ZH + side * ZH + zh) * ROWS,
                )
            )
    for top, bottom, start, _ in blocks:
        for rows, ref in ((top, re_ref), (bottom, im_ref)):
            for chunk in range(CHUNKS):
                cols = slice(chunk * LANES, (chunk + 1) * LANES)
                high, low = split(ref[pl.ds(start + chunk, N_NEAR, stride=ROWS), :])
                xh_ref[rows, cols] = high
                xl_ref[rows, cols] = low
    mixed = dense(xh_ref, xl_ref, high_ref, low_ref)
    for top, bottom, _, start in blocks:
        for chunk in range(CHUNKS):
            cols = slice(chunk * LANES, (chunk + 1) * LANES)
            sine_cols = slice(T + chunk * LANES, T + (chunk + 1) * LANES)
            value = (
                mixed[top, cols] + mixed[bottom, sine_cols],
                mixed[bottom, cols] - mixed[top, sine_cols],
            )
            response = (
                in_ref[pl.ds(start + chunk, N_NEAR, stride=SEND_B), :],
                in_ref[pl.ds(start + CHUNKS + chunk, N_NEAR, stride=SEND_B), :],
            )
            for rows, part in zip((top, bottom), times(value, response)):
                high, low = split(part)
                xh_ref[rows, cols] = high
                xl_ref[rows, cols] = low
    mixed = dense(xh_ref, xl_ref, high_ref, low_ref)
    for top, bottom, start, _ in blocks:
        for chunk in range(CHUNKS):
            cols = slice(chunk * LANES, (chunk + 1) * LANES)
            sine_cols = slice(T + chunk * LANES, T + (chunk + 1) * LANES)
            place = pl.ds(start + chunk, N_NEAR, stride=ROWS)
            re_ref[place, :] = mixed[top, cols] - mixed[bottom, sine_cols]
            im_ref[place, :] = mixed[bottom, cols] + mixed[top, sine_cols]
    values = []
    for kd in range(D):
        w, zh = freq_place(kd)
        at = (zh * N_NEAR + w) * ROWS
        value = (re_ref[pl.ds(at, ROWS), :], im_ref[pl.ds(at, ROWS), :])
        values.append(times_conj(value, (fast_ref[kd, 0], fast_ref[kd, 1])))
    values = complex_transform(values, 1)
    scale = jnp.where(packed, 1.0 / FULL, 0.5 / FULL)
    for w in range(N_NEAR):
        for zh in range(ZH):
            d = digit(w, zh)
            re, im = times_conj(values[d], (slow_ref[item, d, 0], slow_ref[item, d, 1]))
            summed = jnp.where(upper, re + swap_halves(re), swap_halves(im) - im)
            out_ref[pl.ds(w * SEND_C + zh * ROWS, ROWS), :] = (
                jnp.where(packed, re, summed) * scale
            )


def uncoarse_kernel(in_ref, out_ref):
    upper = upper_rows()
    for zh in range(ZH):
        items = []
        for i in range(A):
            first = in_ref[pl.ds(2 * i * SEND_C + zh * ROWS, ROWS), :]
            second = in_ref[pl.ds((2 * i + 1) * SEND_C + zh * ROWS, ROWS), :]
            items.append(regroup(first, second, upper))
        freqs = [(items[0][0], None)] + items[1:] + [(items[0][1], None)]
        for a, value in enumerate(real_inverse(freqs)):
            out_ref[pl.ds((a * ZH + zh) * ROWS, ROWS), :] = value


def gate_kernel(in_ref, q_ref, k_ref, v_ref, gain_hbm, out_ref, gain_ref, sem):
    copy = pltpu.make_async_copy(gain_hbm, gain_ref, sem)
    copy.start()
    channels = q_ref.shape[0]
    row = lax.broadcasted_iota(jnp.int32, (channels, channels), 0)
    col = lax.broadcasted_iota(jnp.int32, (channels, channels), 1)
    product = k_ref[...].astype(jnp.float32) * v_ref[...].astype(jnp.float32)
    convolved = jnp.concatenate(
        [
            jnp.concatenate(
                [
                    in_ref[pl.ds(half * CHUNKS + chunk, N_FAR, stride=ROWS), :]
                    for chunk in range(CHUNKS)
                ],
                axis=1,
            )
            for half in range(2)
        ],
        axis=0,
    )
    copy.wait()
    spread = jnp.broadcast_to(gain_ref[...], (channels, channels))
    gain = jnp.sum(jnp.where(row == col, spread, 0.0), axis=1, keepdims=True)
    gated = q_ref[...].astype(jnp.float32) * (convolved + gain * product)
    out_ref[...] = gated.astype(jnp.bfloat16)


def split_table(table):
    high = table.astype(np.float32).astype(ml_dtypes.bfloat16)
    low = (table - high.astype(np.float64)).astype(np.float32).astype(ml_dtypes.bfloat16)
    return high, low


def tables():
    t = np.arange(T)
    angle = 2 * np.pi * (t[:, None] * t[None, :] % T) / T
    high, low = split_table(np.concatenate([np.cos(angle), np.sin(angle)], axis=1))

    def parts(steps, period):
        angles = 2 * np.pi * (steps % period) / period
        return np.stack([np.cos(angles), -np.sin(angles)], axis=-3).astype(np.float32)

    freqs = np.array([item_freqs(i) for i in range(A)])
    places = np.arange(D * T).reshape(D, 1, T)
    slow = parts(freqs[:, None, :, None] * places, FULL).reshape(A, D, 2, ROWS, LANES)
    fast = parts(np.arange(D)[:, None, None] * t * np.ones((1, 2, 1), int), D * T)
    return slow, fast.reshape(D, 2, ROWS, LANES), high, low


VMEM = pl.BlockSpec(memory_space=pltpu.VMEM)
SMEM = pl.BlockSpec(memory_space=pltpu.SMEM)
HBM = pl.BlockSpec(memory_space=pltpu.HBM)


def call(kernel, shape, in_specs, dtype=jnp.float32, scratch=()):
    return pl.pallas_call(
        kernel,
        out_shape=jax.ShapeDtypeStruct(shape, dtype),
        in_specs=in_specs,
        out_specs=VMEM,
        scratch_shapes=list(scratch),
        compiler_params=pltpu.CompilerParams(vmem_limit_bytes=VMEM_LIMIT),
    )


def run_pack(k_proj, v_proj, spectrum):
    return call(
        pack_kernel,
        (N_FAR * SEND_A, LANES),
        [HBM] * 3,
        scratch=[
            pltpu.VMEM(k_proj.shape, k_proj.dtype),
            pltpu.VMEM(v_proj.shape, v_proj.dtype),
            pltpu.VMEM(spectrum.shape, spectrum.dtype),
            pltpu.SemaphoreType.DMA((3,)),
        ],
    )(k_proj, v_proj, spectrum)


def run_coarse(value):
    return call(coarse_kernel, (N_NEAR * SEND_B, LANES), [VMEM])(value)


def run_filter(item, value):
    return call(
        filter_kernel,
        (N_NEAR * SEND_C, LANES),
        [SMEM] + [VMEM] * 5,
        scratch=[pltpu.VMEM((D * ROWS, LANES), jnp.float32)] * 2
        + [pltpu.VMEM((4 * D, T), jnp.bfloat16)] * 2,
    )(item, value, *tables())


def run_uncoarse(value):
    return call(uncoarse_kernel, (N_FAR * ROWS, LANES), [VMEM])(value)


def run_gate(value, q_proj, k_proj, v_proj, skip_gain):
    return call(
        gate_kernel,
        q_proj.shape,
        [VMEM] * 4 + [HBM],
        dtype=jnp.bfloat16,
        scratch=[pltpu.VMEM((1, q_proj.shape[0]), jnp.float32), pltpu.SemaphoreType.DMA],
    )(value, q_proj, k_proj, v_proj, skip_gain.reshape(1, -1))


def exchange(value, axes, count):
    blocks = value.reshape(count, -1, LANES)
    return lax.all_to_all(blocks, axes, 0, 0, tiled=True).reshape(-1, LANES)


def local(q_proj, k_proj, v_proj, skip_gain, spectrum):
    value = run_pack(k_proj, v_proj, spectrum.reshape(4, *k_proj.shape))
    value = exchange(value, FAR, N_FAR)
    value = run_coarse(value)
    value = exchange(value, NEAR, N_NEAR)
    item = (lax.axis_index(NEAR) // 2).astype(jnp.int32).reshape(1)
    value = run_filter(item, value)
    value = exchange(value, NEAR, N_NEAR)
    value = run_uncoarse(value)
    value = exchange(value, FAR, N_FAR)
    return run_gate(value, q_proj, k_proj, v_proj, skip_gain)


def solution(mesh):
    fine = Mesh(mesh.devices.reshape(SIZES), AXES)
    placed = (P(None, AXES), P(None, AXES), P(None, AXES), P(), P(None, None, None, AXES))
    return jax.shard_map(
        local, mesh=fine, in_specs=placed, out_specs=P(None, AXES), check_vma=False
    )
```

```python
import math

import jax
import jax.numpy as jnp
import ml_dtypes
import numpy as np
from jax import lax
from jax.experimental import pallas as pl
from jax.experimental.pallas import tpu as pltpu
from jax.sharding import Mesh, PartitionSpec as P

AXES = ("xl", "yh", "yl", "core", "xh", "zh", "zl")
SIZES = (2, 4, 2, 2, 2, 4, 2)
FAR = ("xl", "yh", "zh")
NEAR = ("yl", "core", "xh", "zl")
A = 8
ZH = 4
N_FAR = A * ZH
N_NEAR = 16
D = 64
T = 512
LANES = 128
CHUNKS = T // LANES
ROWS = 2 * CHUNKS
FULL = 2 * A * D * T
VMEM_LIMIT = 24 * 1024 * 1024
PACK_LIMIT = 63 * 1024 * 1024


def item_freqs(i):
    return (0, 8) if i == 0 else (i, 16 - i)


def source_of(q):
    xl, y2, y1 = q >> 1 & 1, q >> 2 & 1, q >> 3 & 1
    return q & 1, xl * 4 + y2 * 2 + y1


def digit(w, zh):
    return (w >> 1) * 8 + zh * 2 + (w & 1)


def freq_place(kd):
    y0, core, z0, z1, z2, xh = (kd >> bit & 1 for bit in range(6))
    return y0 * 8 + core * 4 + xh * 2 + z0, z2 * 2 + z1


def add(a, b):
    if a is None:
        return b
    return a if b is None else a + b


def sub(a, b):
    if b is None:
        return a
    return -b if a is None else a - b


def twist(value, steps, period):
    re, im = value
    eighth = 8 * steps % (8 * period)
    if eighth == 0:
        return value
    if eighth == 2 * period:
        return -im, re
    if eighth == 4 * period:
        return -re, -im
    if eighth == 6 * period:
        return im, -re
    c = math.cos(2 * math.pi * steps / period)
    s = math.sin(2 * math.pi * steps / period)
    if abs(abs(c) - abs(s)) < 1e-12:
        r = math.sqrt(0.5)
        cs, ss = math.copysign(1.0, c), math.copysign(1.0, s)
        a = re if cs > 0 else -re
        b = im if cs > 0 else -im
        return (
            ((a - im) if ss > 0 else (a + im)) * r,
            ((b + re) if ss > 0 else (b - re)) * r,
        )
    return re * c - im * s, re * s + im * c


def real_forward(x):
    n = len(x)
    if n == 2:
        return [(add(x[0], x[1]), None), (sub(x[0], x[1]), None)]
    even, odd = real_forward(x[0::2]), real_forward(x[1::2])
    out = [None] * (n // 2 + 1)
    out[0] = (even[0][0] + odd[0][0], None)
    out[n // 2] = (even[0][0] - odd[0][0], None)
    out[n // 4] = (even[n // 4][0], -odd[n // 4][0])
    for k in range(1, n // 4):
        tr, ti = twist(odd[k], -k, n)
        er, ei = even[k]
        out[k] = (er + tr, ei + ti)
        out[n // 2 - k] = (er - tr, ti - ei)
    return out


def real_inverse(x):
    n = 2 * (len(x) - 1)
    if n == 2:
        return [x[0][0] + x[1][0]]
    even, odd = [None] * (n // 4 + 1), [None] * (n // 4 + 1)
    even[0] = (x[0][0] + x[n // 2][0], None)
    odd[0] = (x[0][0] - x[n // 2][0], None)
    even[n // 4] = (2.0 * x[n // 4][0], None)
    odd[n // 4] = (-2.0 * x[n // 4][1], None)
    for k in range(1, n // 4):
        ar, ai = x[k]
        br, bi = x[n // 2 - k]
        even[k] = (ar + br, ai - bi)
        odd[k] = twist((ar - br, ai + bi), k, n)
    out = [None] * (n // 2)
    out[0::2], out[1::2] = real_inverse(even), real_inverse(odd)
    return out


def complex_transform(x, sign):
    n = len(x)
    if n == 1:
        return x
    even, odd = complex_transform(x[0::2], sign), complex_transform(x[1::2], sign)
    low, high = [], []
    for k in range(n // 2):
        tr, ti = twist(odd[k], sign * k, n)
        er, ei = even[k]
        low.append((er + tr, ei + ti))
        high.append((er - tr, ei - ti))
    return low + high


def times(a, b):
    return a[0] * b[0] - a[1] * b[1], a[0] * b[1] + a[1] * b[0]


def times_conj(a, b):
    return a[0] * b[0] + a[1] * b[1], a[1] * b[0] - a[0] * b[1]


SEND_A = 5 * ROWS
SEND_B = 12 * ROWS
SEND_C = 4 * ROWS


def pack_kernel(k_hbm, v_hbm, spec_hbm, out_ref, k_ref, v_ref, spec_ref, sems):
    copies = [
        pltpu.make_async_copy(source, target, sems.at[i])
        for i, (source, target) in enumerate(
            ((k_hbm, k_ref), (v_hbm, v_ref), (spec_hbm, spec_ref))
        )
    ]
    for copy in copies:
        copy.start()
    copies[0].wait()
    copies[1].wait()
    product = k_ref[...].astype(jnp.float32) * v_ref[...].astype(jnp.float32)
    for half in range(2):
        rows = slice(half * N_FAR, (half + 1) * N_FAR)
        for chunk in range(CHUNKS):
            cols = slice(chunk * LANES, (chunk + 1) * LANES)
            place = half * CHUNKS + chunk
            out_ref[pl.ds(place, N_FAR, stride=SEND_A), :] = product[rows, cols]
    copies[2].wait()
    for half in range(2):
        rows = slice(half * N_FAR, (half + 1) * N_FAR)
        for chunk in range(CHUNKS):
            cols = slice(chunk * LANES, (chunk + 1) * LANES)
            for parity in range(2):
                for part in range(2):
                    place = (1 + 2 * parity + half) * ROWS + part * CHUNKS + chunk
                    out_ref[pl.ds(place, N_FAR, stride=SEND_A), :] = spec_ref[
                        2 * parity + part, rows, cols
                    ]


def upper_rows():
    return lax.broadcasted_iota(jnp.int32, (ROWS, LANES), 0) < CHUNKS


def swap_halves(value):
    return pltpu.roll(value, CHUNKS, 0)


def regroup(first, second, upper):
    return (
        jnp.where(upper, first, swap_halves(second)),
        jnp.where(upper, swap_halves(first), second),
    )


def coarse_kernel(in_ref, out_ref):
    upper = upper_rows()
    for zh in range(ZH):
        tokens = [in_ref[pl.ds((a * ZH + zh) * SEND_A, ROWS), :] for a in range(A)]
        freqs = real_forward(tokens + [None] * A)
        items = [(freqs[0][0], freqs[A][0])] + freqs[1:A]
        for i in range(A):
            for ch, value in enumerate(regroup(items[i][0], items[i][1], upper)):
                base = (2 * i + ch) * SEND_B
                out_ref[pl.ds(base + zh * ROWS, ROWS), :] = value
                for side, q in enumerate(item_freqs(i)):
                    parity, a = source_of(q)
                    source = (a * ZH + zh) * SEND_A + (1 + 2 * parity + ch) * ROWS
                    target = base + (ZH + side * ZH + zh) * ROWS
                    out_ref[pl.ds(target, ROWS), :] = in_ref[pl.ds(source, ROWS), :]


def split(value):
    high = value.astype(jnp.bfloat16)
    return high, (value - high.astype(jnp.float32)).astype(jnp.bfloat16)


def dense(high_ref, low_ref, table_ref):
    def dot(ref, first):
        table = table_ref[first : first + T, :]
        return jnp.dot(ref[...], table, preferred_element_type=jnp.float32)

    return dot(high_ref, 0) + (dot(low_ref, 0) + dot(high_ref, T))


def filter_kernel(
    i_ref, in_ref, turn_ref, table_ref, out_ref, re_ref, im_ref, xh_ref, xl_ref
):
    item = i_ref[0]
    packed = item == 0
    upper = upper_rows()
    keep = jnp.logical_or(upper, packed)
    signs = jnp.where(upper, 1.0, -1.0) * jnp.where(packed, 0.0, 1.0)
    values = [None] * D
    for w in range(N_NEAR):
        for zh in range(ZH):
            d = digit(w, zh)
            value = in_ref[pl.ds(w * SEND_B + zh * ROWS, ROWS), :]
            other = swap_halves(value)
            pair = (jnp.where(keep, value, other), jnp.where(upper, other, value) * signs)
            values[d] = times(pair, (turn_ref[d, 0], turn_ref[d, 1]))
    for kd, value in enumerate(complex_transform(values, -1)):
        w, zh = freq_place(kd)
        at = (zh * N_NEAR + w) * ROWS
        re_ref[pl.ds(at, ROWS), :], im_ref[pl.ds(at, ROWS), :] = times(
            value, (turn_ref[D + kd, 0], turn_ref[D + kd, 1])
        )
    half_rows = 2 * D
    blocks = []
    for side in range(2):
        for zh in range(ZH):
            first = (side * ZH + zh) * N_NEAR
            blocks.append(
                (
                    slice(first, first + N_NEAR),
                    slice(half_rows + first, half_rows + first + N_NEAR),
                    zh * N_NEAR * ROWS + side * CHUNKS,
                    (ZH + side * ZH + zh) * ROWS,
                )
            )
    for top, bottom, start, _ in blocks:
        for rows, ref in ((top, re_ref), (bottom, im_ref)):
            for chunk in range(CHUNKS):
                cols = slice(chunk * LANES, (chunk + 1) * LANES)
                high, low = split(ref[pl.ds(start + chunk, N_NEAR, stride=ROWS), :])
                xh_ref[rows, cols] = high
                xl_ref[rows, cols] = low
    mixed = dense(xh_ref, xl_ref, table_ref)
    for top, bottom, _, start in blocks:
        for chunk in range(CHUNKS):
            cols = slice(chunk * LANES, (chunk + 1) * LANES)
            sine_cols = slice(T + chunk * LANES, T + (chunk + 1) * LANES)
            value = (
                mixed[top, cols] + mixed[bottom, sine_cols],
                mixed[bottom, cols] - mixed[top, sine_cols],
            )
            response = (
                in_ref[pl.ds(start + chunk, N_NEAR, stride=SEND_B), :],
                in_ref[pl.ds(start + CHUNKS + chunk, N_NEAR, stride=SEND_B), :],
            )
            for rows, part in zip((top, bottom), times(value, response)):
                high, low = split(part)
                xh_ref[rows, cols] = high
                xl_ref[rows, cols] = low
    mixed = dense(xh_ref, xl_ref, table_ref)
    for top, bottom, start, _ in blocks:
        for chunk in range(CHUNKS):
            cols = slice(chunk * LANES, (chunk + 1) * LANES)
            sine_cols = slice(T + chunk * LANES, T + (chunk + 1) * LANES)
            place = pl.ds(start + chunk, N_NEAR, stride=ROWS)
            re_ref[place, :] = mixed[top, cols] - mixed[bottom, sine_cols]
            im_ref[place, :] = mixed[bottom, cols] + mixed[top, sine_cols]
    values = []
    for kd in range(D):
        w, zh = freq_place(kd)
        at = (zh * N_NEAR + w) * ROWS
        value = (re_ref[pl.ds(at, ROWS), :], im_ref[pl.ds(at, ROWS), :])
        values.append(times_conj(value, (turn_ref[D + kd, 0], turn_ref[D + kd, 1])))
    values = complex_transform(values, 1)
    scale = jnp.where(packed, 1.0 / FULL, 0.5 / FULL)
    for w in range(N_NEAR):
        for zh in range(ZH):
            d = digit(w, zh)
            re, im = times_conj(values[d], (turn_ref[d, 0], turn_ref[d, 1]))
            summed = jnp.where(upper, re + swap_halves(re), swap_halves(im) - im)
            out_ref[pl.ds(w * SEND_C + zh * ROWS, ROWS), :] = (
                jnp.where(packed, re, summed) * scale
            )


def uncoarse_kernel(in_ref, out_ref):
    upper = upper_rows()
    for zh in range(ZH):
        items = []
        for i in range(A):
            first = in_ref[pl.ds(2 * i * SEND_C + zh * ROWS, ROWS), :]
            second = in_ref[pl.ds((2 * i + 1) * SEND_C + zh * ROWS, ROWS), :]
            items.append(regroup(first, second, upper))
        freqs = [(items[0][0], None)] + items[1:] + [(items[0][1], None)]
        for a, value in enumerate(real_inverse(freqs)):
            out_ref[pl.ds((a * ZH + zh) * ROWS, ROWS), :] = value


def gate_kernel(in_ref, q_ref, k_ref, v_ref, gain_hbm, out_ref, gain_ref, sem):
    copy = pltpu.make_async_copy(gain_hbm, gain_ref, sem)
    copy.start()
    channels = q_ref.shape[0]
    row = lax.broadcasted_iota(jnp.int32, (channels, channels), 0)
    col = lax.broadcasted_iota(jnp.int32, (channels, channels), 1)
    product = k_ref[...].astype(jnp.float32) * v_ref[...].astype(jnp.float32)
    convolved = jnp.concatenate(
        [
            jnp.concatenate(
                [
                    in_ref[pl.ds(half * CHUNKS + chunk, N_FAR, stride=ROWS), :]
                    for chunk in range(CHUNKS)
                ],
                axis=1,
            )
            for half in range(2)
        ],
        axis=0,
    )
    copy.wait()
    spread = jnp.broadcast_to(gain_ref[...], (channels, channels))
    gain = jnp.sum(jnp.where(row == col, spread, 0.0), axis=1, keepdims=True)
    gated = q_ref[...].astype(jnp.float32) * (convolved + gain * product)
    out_ref[...] = gated.astype(jnp.bfloat16)


def split_table(table):
    high = table.astype(np.float32).astype(ml_dtypes.bfloat16)
    low = (table - high.astype(np.float64)).astype(np.float32).astype(ml_dtypes.bfloat16)
    return high, low


def tables():
    t = np.arange(T)
    angle = 2 * np.pi * (t[:, None] * t[None, :] % T) / T
    high, low = split_table(np.concatenate([np.cos(angle), np.sin(angle)], axis=1))

    def parts(steps, period):
        angles = 2 * np.pi * (steps % period) / period
        return np.stack([np.cos(angles), -np.sin(angles)], axis=-3).astype(np.float32)

    freqs = np.array([item_freqs(i) for i in range(A)])
    places = np.arange(D * T).reshape(D, 1, T)
    slow = parts(freqs[:, None, :, None] * places, FULL).reshape(A, D, 2, ROWS, LANES)
    fast = parts(np.arange(D)[:, None, None] * t * np.ones((1, 2, 1), int), D * T)
    fast = np.broadcast_to(fast.reshape(1, D, 2, ROWS, LANES), slow.shape)
    return np.concatenate([slow, fast], axis=1), high, low


VMEM = pl.BlockSpec(memory_space=pltpu.VMEM)
SMEM = pl.BlockSpec(memory_space=pltpu.SMEM)
HBM = pl.BlockSpec(memory_space=pltpu.HBM)


def call(kernel, shape, in_specs, dtype=jnp.float32, scratch=(), limit=VMEM_LIMIT):
    return pl.pallas_call(
        kernel,
        out_shape=jax.ShapeDtypeStruct(shape, dtype),
        in_specs=in_specs,
        out_specs=VMEM,
        scratch_shapes=list(scratch),
        compiler_params=pltpu.CompilerParams(vmem_limit_bytes=limit),
    )


def run_pack(k_proj, v_proj, spectrum):
    return call(
        pack_kernel,
        (N_FAR * SEND_A, LANES),
        [HBM] * 3,
        scratch=[
            pltpu.VMEM(k_proj.shape, k_proj.dtype),
            pltpu.VMEM(v_proj.shape, v_proj.dtype),
            pltpu.VMEM(spectrum.shape, spectrum.dtype),
            pltpu.SemaphoreType.DMA((3,)),
        ],
        limit=PACK_LIMIT,
    )(k_proj, v_proj, spectrum)


def run_coarse(value):
    return call(coarse_kernel, (N_NEAR * SEND_B, LANES), [VMEM])(value)


def run_filter(item, value):
    turns, high, low = tables()
    turns = lax.dynamic_index_in_dim(turns, item[0], keepdims=False)
    dense_table = lax.dynamic_index_in_dim(
        np.stack([np.concatenate([high, low])] * 2), item[0] % 2, keepdims=False
    )
    return call(
        filter_kernel,
        (N_NEAR * SEND_C, LANES),
        [SMEM] + [VMEM] * 3,
        scratch=[pltpu.VMEM((D * ROWS, LANES), jnp.float32)] * 2
        + [pltpu.VMEM((4 * D, T), jnp.bfloat16)] * 2,
    )(item, value, turns, dense_table)


def run_uncoarse(value):
    return call(uncoarse_kernel, (N_FAR * ROWS, LANES), [VMEM])(value)


def run_gate(value, q_proj, k_proj, v_proj, skip_gain):
    return call(
        gate_kernel,
        q_proj.shape,
        [VMEM] * 4 + [HBM],
        dtype=jnp.bfloat16,
        scratch=[pltpu.VMEM((1, q_proj.shape[0]), jnp.float32), pltpu.SemaphoreType.DMA],
    )(value, q_proj, k_proj, v_proj, skip_gain.reshape(1, -1))


def exchange(value, axes, count):
    blocks = value.reshape(count, -1, LANES)
    return lax.all_to_all(blocks, axes, 0, 0, tiled=True).reshape(-1, LANES)


def local(q_proj, k_proj, v_proj, skip_gain, spectrum):
    value = run_pack(k_proj, v_proj, spectrum.reshape(4, *k_proj.shape))
    value = exchange(value, FAR, N_FAR)
    value = run_coarse(value)
    value = exchange(value, NEAR, N_NEAR)
    item = (lax.axis_index(NEAR) // 2).astype(jnp.int32).reshape(1)
    value = run_filter(item, value)
    value = exchange(value, NEAR, N_NEAR)
    value = run_uncoarse(value)
    value = exchange(value, FAR, N_FAR)
    return run_gate(value, q_proj, k_proj, v_proj, skip_gain)


def solution(mesh):
    fine = Mesh(mesh.devices.reshape(SIZES), AXES)
    placed = (P(None, AXES), P(None, AXES), P(None, AXES), P(), P(None, None, None, AXES))
    return jax.shard_map(
        local, mesh=fine, in_specs=placed, out_specs=P(None, AXES), check_vma=False
    )
```

```python
import math

import jax
import jax.numpy as jnp
import ml_dtypes
import numpy as np
from jax import lax
from jax.experimental import pallas as pl
from jax.experimental.pallas import tpu as pltpu
from jax.sharding import Mesh, PartitionSpec as P

AXES = ("xl", "yh", "yl", "core", "xh", "zh", "zl")
SIZES = (2, 4, 2, 2, 2, 4, 2)
FAR = ("xl", "yh", "zh")
NEAR = ("yl", "core", "xh", "zl")
A = 8
ZH = 4
N_FAR = A * ZH
N_NEAR = 16
D = 64
T = 512
LANES = 128
CHUNKS = T // LANES
ROWS = 2 * CHUNKS
FULL = 2 * A * D * T
VMEM_LIMIT = 12 * 1024 * 1024


def item_freqs(i):
    return (0, 8) if i == 0 else (i, 16 - i)


def source_of(q):
    xl, y2, y1 = q >> 1 & 1, q >> 2 & 1, q >> 3 & 1
    return q & 1, xl * 4 + y2 * 2 + y1


def digit(w, zh):
    return (w >> 1) * 8 + zh * 2 + (w & 1)


def freq_place(kd):
    y0, core, z0, z1, z2, xh = (kd >> bit & 1 for bit in range(6))
    return y0 * 8 + core * 4 + xh * 2 + z0, z2 * 2 + z1


def add(a, b):
    if a is None:
        return b
    return a if b is None else a + b


def sub(a, b):
    if b is None:
        return a
    return -b if a is None else a - b


def twist(value, steps, period):
    re, im = value
    eighth = 8 * steps % (8 * period)
    if eighth == 0:
        return value
    if eighth == 2 * period:
        return -im, re
    if eighth == 4 * period:
        return -re, -im
    if eighth == 6 * period:
        return im, -re
    c = math.cos(2 * math.pi * steps / period)
    s = math.sin(2 * math.pi * steps / period)
    if abs(abs(c) - abs(s)) < 1e-12:
        r = math.sqrt(0.5)
        cs, ss = math.copysign(1.0, c), math.copysign(1.0, s)
        a = re if cs > 0 else -re
        b = im if cs > 0 else -im
        return (
            ((a - im) if ss > 0 else (a + im)) * r,
            ((b + re) if ss > 0 else (b - re)) * r,
        )
    return re * c - im * s, re * s + im * c


def real_forward(x):
    n = len(x)
    if n == 2:
        return [(add(x[0], x[1]), None), (sub(x[0], x[1]), None)]
    even, odd = real_forward(x[0::2]), real_forward(x[1::2])
    out = [None] * (n // 2 + 1)
    out[0] = (even[0][0] + odd[0][0], None)
    out[n // 2] = (even[0][0] - odd[0][0], None)
    out[n // 4] = (even[n // 4][0], -odd[n // 4][0])
    for k in range(1, n // 4):
        tr, ti = twist(odd[k], -k, n)
        er, ei = even[k]
        out[k] = (er + tr, ei + ti)
        out[n // 2 - k] = (er - tr, ti - ei)
    return out


def real_inverse(x):
    n = 2 * (len(x) - 1)
    if n == 2:
        return [x[0][0] + x[1][0]]
    even, odd = [None] * (n // 4 + 1), [None] * (n // 4 + 1)
    even[0] = (x[0][0] + x[n // 2][0], None)
    odd[0] = (x[0][0] - x[n // 2][0], None)
    even[n // 4] = (2.0 * x[n // 4][0], None)
    odd[n // 4] = (-2.0 * x[n // 4][1], None)
    for k in range(1, n // 4):
        ar, ai = x[k]
        br, bi = x[n // 2 - k]
        even[k] = (ar + br, ai - bi)
        odd[k] = twist((ar - br, ai + bi), k, n)
    out = [None] * (n // 2)
    out[0::2], out[1::2] = real_inverse(even), real_inverse(odd)
    return out


def complex_transform(x, sign):
    n = len(x)
    if n == 1:
        return x
    even, odd = complex_transform(x[0::2], sign), complex_transform(x[1::2], sign)
    low, high = [], []
    for k in range(n // 2):
        tr, ti = twist(odd[k], sign * k, n)
        er, ei = even[k]
        low.append((er + tr, ei + ti))
        high.append((er - tr, ei - ti))
    return low + high


def times(a, b):
    return a[0] * b[0] - a[1] * b[1], a[0] * b[1] + a[1] * b[0]


def times_conj(a, b):
    return a[0] * b[0] + a[1] * b[1], a[1] * b[0] - a[0] * b[1]


SEND_A = 5 * ROWS
SEND_B = 12 * ROWS
SEND_C = 4 * ROWS


def pack_kernel(k_hbm, v_hbm, spec_hbm, out_ref, k_ref, v_ref, spec_ref, sems):
    copies = [
        pltpu.make_async_copy(source, target, sems.at[i])
        for i, (source, target) in enumerate(
            ((k_hbm, k_ref), (v_hbm, v_ref), (spec_hbm, spec_ref))
        )
    ]
    for copy in copies:
        copy.start()
    copies[0].wait()
    copies[1].wait()
    product = k_ref[...].astype(jnp.float32) * v_ref[...].astype(jnp.float32)
    for half in range(2):
        rows = slice(half * N_FAR, (half + 1) * N_FAR)
        for chunk in range(CHUNKS):
            cols = slice(chunk * LANES, (chunk + 1) * LANES)
            place = half * CHUNKS + chunk
            out_ref[pl.ds(place, N_FAR, stride=SEND_A), :] = product[rows, cols]
    copies[2].wait()
    for half in range(2):
        rows = slice(half * N_FAR, (half + 1) * N_FAR)
        for chunk in range(CHUNKS):
            cols = slice(chunk * LANES, (chunk + 1) * LANES)
            for parity in range(2):
                for part in range(2):
                    place = (1 + 2 * parity + half) * ROWS + part * CHUNKS + chunk
                    out_ref[pl.ds(place, N_FAR, stride=SEND_A), :] = spec_ref[
                        2 * parity + part, rows, cols
                    ]


def upper_rows():
    return lax.broadcasted_iota(jnp.int32, (ROWS, LANES), 0) < CHUNKS


def swap_halves(value):
    return pltpu.roll(value, CHUNKS, 0)


def regroup(first, second, upper):
    return (
        jnp.where(upper, first, swap_halves(second)),
        jnp.where(upper, swap_halves(first), second),
    )


def coarse_kernel(in_ref, out_ref):
    upper = upper_rows()
    for zh in range(ZH):
        tokens = [in_ref[pl.ds((a * ZH + zh) * SEND_A, ROWS), :] for a in range(A)]
        freqs = real_forward(tokens + [None] * A)
        items = [(freqs[0][0], freqs[A][0])] + freqs[1:A]
        for i in range(A):
            for ch, value in enumerate(regroup(items[i][0], items[i][1], upper)):
                base = (2 * i + ch) * SEND_B
                out_ref[pl.ds(base + zh * ROWS, ROWS), :] = value
                for side, q in enumerate(item_freqs(i)):
                    parity, a = source_of(q)
                    source = (a * ZH + zh) * SEND_A + (1 + 2 * parity + ch) * ROWS
                    target = base + (ZH + side * ZH + zh) * ROWS
                    out_ref[pl.ds(target, ROWS), :] = in_ref[pl.ds(source, ROWS), :]


def split(value):
    high = value.astype(jnp.bfloat16)
    return high, (value - high.astype(jnp.float32)).astype(jnp.bfloat16)


def dense(high_ref, low_ref, table_ref):
    def dot(ref, first):
        table = table_ref[first : first + T, :]
        return jnp.dot(ref[...], table, preferred_element_type=jnp.float32)

    return dot(high_ref, 0) + (dot(low_ref, 0) + dot(high_ref, T))


def filter_kernel(
    i_ref, in_ref, slow_ref, fast_hbm, table_hbm, out_ref,
    re_ref, im_ref, xh_ref, xl_ref, fast_ref, table_ref, sems,
):
    fast_copy = pltpu.make_async_copy(fast_hbm, fast_ref, sems.at[0])
    table_copy = pltpu.make_async_copy(table_hbm, table_ref, sems.at[1])
    fast_copy.start()
    table_copy.start()
    item = i_ref[0]
    packed = item == 0
    upper = upper_rows()
    keep = jnp.logical_or(upper, packed)
    signs = jnp.where(upper, 1.0, -1.0) * jnp.where(packed, 0.0, 1.0)
    values = [None] * D
    for w in range(N_NEAR):
        for zh in range(ZH):
            d = digit(w, zh)
            value = in_ref[pl.ds(w * SEND_B + zh * ROWS, ROWS), :]
            other = swap_halves(value)
            pair = (jnp.where(keep, value, other), jnp.where(upper, other, value) * signs)
            values[d] = times(pair, (slow_ref[d, 0], slow_ref[d, 1]))
    fast_copy.wait()
    for kd, value in enumerate(complex_transform(values, -1)):
        w, zh = freq_place(kd)
        at = (zh * N_NEAR + w) * ROWS
        re_ref[pl.ds(at, ROWS), :], im_ref[pl.ds(at, ROWS), :] = times(
            value, (fast_ref[kd, 0], fast_ref[kd, 1])
        )
    half_rows = 2 * D
    blocks = []
    for side in range(2):
        for zh in range(ZH):
            first = (side * ZH + zh) * N_NEAR
            blocks.append(
                (
                    slice(first, first + N_NEAR),
                    slice(half_rows + first, half_rows + first + N_NEAR),
                    zh * N_NEAR * ROWS + side * CHUNKS,
                    (ZH + side * ZH + zh) * ROWS,
                )
            )
    for top, bottom, start, _ in blocks:
        for rows, ref in ((top, re_ref), (bottom, im_ref)):
            for chunk in range(CHUNKS):
                cols = slice(chunk * LANES, (chunk + 1) * LANES)
                high, low = split(ref[pl.ds(start + chunk, N_NEAR, stride=ROWS), :])
                xh_ref[rows, cols] = high
                xl_ref[rows, cols] = low
    table_copy.wait()
    mixed = dense(xh_ref, xl_ref, table_ref)
    for top, bottom, _, start in blocks:
        for chunk in range(CHUNKS):
            cols = slice(chunk * LANES, (chunk + 1) * LANES)
            sine_cols = slice(T + chunk * LANES, T + (chunk + 1) * LANES)
            value = (
                mixed[top, cols] + mixed[bottom, sine_cols],
                mixed[bottom, cols] - mixed[top, sine_cols],
            )
            response = (
                in_ref[pl.ds(start + chunk, N_NEAR, stride=SEND_B), :],
                in_ref[pl.ds(start + CHUNKS + chunk, N_NEAR, stride=SEND_B), :],
            )
            for rows, part in zip((top, bottom), times(value, response)):
                high, low = split(part)
                xh_ref[rows, cols] = high
                xl_ref[rows, cols] = low
    mixed = dense(xh_ref, xl_ref, table_ref)
    for top, bottom, start, _ in blocks:
        for chunk in range(CHUNKS):
            cols = slice(chunk * LANES, (chunk + 1) * LANES)
            sine_cols = slice(T + chunk * LANES, T + (chunk + 1) * LANES)
            place = pl.ds(start + chunk, N_NEAR, stride=ROWS)
            re_ref[place, :] = mixed[top, cols] - mixed[bottom, sine_cols]
            im_ref[place, :] = mixed[bottom, cols] + mixed[top, sine_cols]
    values = []
    for kd in range(D):
        w, zh = freq_place(kd)
        at = (zh * N_NEAR + w) * ROWS
        value = (re_ref[pl.ds(at, ROWS), :], im_ref[pl.ds(at, ROWS), :])
        values.append(times_conj(value, (fast_ref[kd, 0], fast_ref[kd, 1])))
    values = complex_transform(values, 1)
    scale = jnp.where(packed, 1.0 / FULL, 0.5 / FULL)
    for w in range(N_NEAR):
        for zh in range(ZH):
            d = digit(w, zh)
            re, im = times_conj(values[d], (slow_ref[d, 0], slow_ref[d, 1]))
            summed = jnp.where(upper, re + swap_halves(re), swap_halves(im) - im)
            out_ref[pl.ds(w * SEND_C + zh * ROWS, ROWS), :] = (
                jnp.where(packed, re, summed) * scale
            )


def uncoarse_kernel(in_ref, out_ref):
    upper = upper_rows()
    for zh in range(ZH):
        items = []
        for i in range(A):
            first = in_ref[pl.ds(2 * i * SEND_C + zh * ROWS, ROWS), :]
            second = in_ref[pl.ds((2 * i + 1) * SEND_C + zh * ROWS, ROWS), :]
            items.append(regroup(first, second, upper))
        freqs = [(items[0][0], None)] + items[1:] + [(items[0][1], None)]
        for a, value in enumerate(real_inverse(freqs)):
            out_ref[pl.ds((a * ZH + zh) * ROWS, ROWS), :] = value


def gate_kernel(in_ref, q_ref, k_ref, v_ref, gain_hbm, out_ref, gain_ref, sem):
    copy = pltpu.make_async_copy(gain_hbm, gain_ref, sem)
    copy.start()
    channels = q_ref.shape[0]
    row = lax.broadcasted_iota(jnp.int32, (channels, channels), 0)
    col = lax.broadcasted_iota(jnp.int32, (channels, channels), 1)
    product = k_ref[...].astype(jnp.float32) * v_ref[...].astype(jnp.float32)
    convolved = jnp.concatenate(
        [
            jnp.concatenate(
                [
                    in_ref[pl.ds(half * CHUNKS + chunk, N_FAR, stride=ROWS), :]
                    for chunk in range(CHUNKS)
                ],
                axis=1,
            )
            for half in range(2)
        ],
        axis=0,
    )
    copy.wait()
    spread = jnp.broadcast_to(gain_ref[...], (channels, channels))
    gain = jnp.sum(jnp.where(row == col, spread, 0.0), axis=1, keepdims=True)
    gated = q_ref[...].astype(jnp.float32) * (convolved + gain * product)
    out_ref[...] = gated.astype(jnp.bfloat16)


def split_table(table):
    high = table.astype(np.float32).astype(ml_dtypes.bfloat16)
    low = (table - high.astype(np.float64)).astype(np.float32).astype(ml_dtypes.bfloat16)
    return high, low


def tables():
    t = np.arange(T)
    angle = 2 * np.pi * (t[:, None] * t[None, :] % T) / T
    high, low = split_table(np.concatenate([np.cos(angle), np.sin(angle)], axis=1))

    def parts(steps, period):
        angles = 2 * np.pi * (steps % period) / period
        return np.stack([np.cos(angles), -np.sin(angles)], axis=-3).astype(np.float32)

    freqs = np.array([item_freqs(i) for i in range(A)])
    places = np.arange(D * T).reshape(D, 1, T)
    slow = parts(freqs[:, None, :, None] * places, FULL).reshape(A, D, 2, ROWS, LANES)
    fast = parts(np.arange(D)[:, None, None] * t * np.ones((1, 2, 1), int), D * T)
    return slow, fast.reshape(D, 2, ROWS, LANES), np.concatenate([high, low])


VMEM = pl.BlockSpec(memory_space=pltpu.VMEM)
SMEM = pl.BlockSpec(memory_space=pltpu.SMEM)
HBM = pl.BlockSpec(memory_space=pltpu.HBM)


def in_hbm(x):
    return pltpu.with_memory_space_constraint(jnp.asarray(x), pltpu.HBM)


def call(kernel, shape, in_specs, dtype=jnp.float32, scratch=(), limit=VMEM_LIMIT):
    return pl.pallas_call(
        kernel,
        out_shape=jax.ShapeDtypeStruct(shape, dtype),
        in_specs=in_specs,
        out_specs=VMEM,
        scratch_shapes=list(scratch),
        compiler_params=pltpu.CompilerParams(vmem_limit_bytes=limit),
    )


def run_pack(k_proj, v_proj, spectrum):
    return call(
        pack_kernel,
        (N_FAR * SEND_A, LANES),
        [HBM] * 3,
        scratch=[
            pltpu.VMEM(k_proj.shape, k_proj.dtype),
            pltpu.VMEM(v_proj.shape, v_proj.dtype),
            pltpu.VMEM(spectrum.shape, spectrum.dtype),
            pltpu.SemaphoreType.DMA((3,)),
        ],
    )(*(in_hbm(x) for x in (k_proj, v_proj, spectrum)))


def run_coarse(value):
    return call(coarse_kernel, (N_NEAR * SEND_B, LANES), [VMEM])(value)


def run_filter(item, value):
    slow, fast, table = tables()
    slow = lax.dynamic_index_in_dim(slow, item[0], keepdims=False)
    return call(
        filter_kernel,
        (N_NEAR * SEND_C, LANES),
        [SMEM] + [VMEM] * 2 + [HBM] * 2,
        scratch=[pltpu.VMEM((D * ROWS, LANES), jnp.float32)] * 2
        + [pltpu.VMEM((4 * D, T), jnp.bfloat16)] * 2
        + [
            pltpu.VMEM(fast.shape, jnp.float32),
            pltpu.VMEM(table.shape, jnp.bfloat16),
            pltpu.SemaphoreType.DMA((2,)),
        ],
    )(item, value, slow, *(in_hbm(x) for x in (fast, table)))


def run_uncoarse(value):
    return call(uncoarse_kernel, (N_FAR * ROWS, LANES), [VMEM])(value)


def run_gate(value, q_proj, k_proj, v_proj, skip_gain):
    return call(
        gate_kernel,
        q_proj.shape,
        [VMEM] * 4 + [HBM],
        dtype=jnp.bfloat16,
        scratch=[pltpu.VMEM((1, q_proj.shape[0]), jnp.float32), pltpu.SemaphoreType.DMA],
    )(value, q_proj, k_proj, v_proj, skip_gain.reshape(1, -1))


def exchange(value, axes, count):
    blocks = value.reshape(count, -1, LANES)
    return lax.all_to_all(blocks, axes, 0, 0, tiled=True).reshape(-1, LANES)


def local(q_proj, k_proj, v_proj, skip_gain, spectrum):
    value = run_pack(k_proj, v_proj, spectrum.reshape(4, *k_proj.shape))
    value = exchange(value, FAR, N_FAR)
    value = run_coarse(value)
    value = exchange(value, NEAR, N_NEAR)
    item = (lax.axis_index(NEAR) // 2).astype(jnp.int32).reshape(1)
    value = run_filter(item, value)
    value = exchange(value, NEAR, N_NEAR)
    value = run_uncoarse(value)
    value = exchange(value, FAR, N_FAR)
    return run_gate(value, q_proj, k_proj, v_proj, skip_gain)


def solution(mesh):
    fine = Mesh(mesh.devices.reshape(SIZES), AXES)
    placed = (P(None, AXES), P(None, AXES), P(None, AXES), P(), P(None, None, None, AXES))
    return jax.shard_map(
        local, mesh=fine, in_specs=placed, out_specs=P(None, AXES), check_vma=False
    )
```

```python
import math

import jax
import jax.numpy as jnp
import ml_dtypes
import numpy as np
from jax import lax
from jax.experimental import pallas as pl
from jax.experimental.pallas import tpu as pltpu
from jax.sharding import Mesh, PartitionSpec as P

AXES = ("xl", "yh", "yl", "core", "xh", "zh", "zl")
SIZES = (2, 4, 2, 2, 2, 4, 2)
FAR = ("xl", "yh", "yl", "zh")
NEAR = ("core", "xh", "zl")
A = 8
B = 8
N_FAR = A * B
N_NEAR = 8
D = B * N_NEAR
T = 512
LANES = 128
CHUNKS = T // LANES
ROWS = 2 * CHUNKS
FULL = 2 * A * D * T
VMEM_LIMIT = 12 * 1024 * 1024


def item_freqs(i):
    return (0, 8) if i == 0 else (i, 16 - i)


def source_of(q):
    xl, y2, y1 = q >> 1 & 1, q >> 2 & 1, q >> 3 & 1
    return q & 1, xl * 4 + y2 * 2 + y1


def digit(w, b):
    core, xh, zl = w >> 2, w >> 1 & 1, w & 1
    yl, zh = b >> 2, b & 3
    return yl * 32 + core * 16 + xh * 8 + zh * 2 + zl


def freq_place(kd):
    y0, core, z0, z1, z2, xh = (kd >> bit & 1 for bit in range(6))
    return core * 4 + xh * 2 + z0, y0 * 4 + z2 * 2 + z1


def add(a, b):
    if a is None:
        return b
    return a if b is None else a + b


def sub(a, b):
    if b is None:
        return a
    return -b if a is None else a - b


def twist(value, steps, period):
    re, im = value
    eighth = 8 * steps % (8 * period)
    if eighth == 0:
        return value
    if eighth == 2 * period:
        return -im, re
    if eighth == 4 * period:
        return -re, -im
    if eighth == 6 * period:
        return im, -re
    c = math.cos(2 * math.pi * steps / period)
    s = math.sin(2 * math.pi * steps / period)
    if abs(abs(c) - abs(s)) < 1e-12:
        r = math.sqrt(0.5)
        cs, ss = math.copysign(1.0, c), math.copysign(1.0, s)
        a = re if cs > 0 else -re
        b = im if cs > 0 else -im
        return (
            ((a - im) if ss > 0 else (a + im)) * r,
            ((b + re) if ss > 0 else (b - re)) * r,
        )
    return re * c - im * s, re * s + im * c


def real_forward(x):
    n = len(x)
    if n == 2:
        return [(add(x[0], x[1]), None), (sub(x[0], x[1]), None)]
    even, odd = real_forward(x[0::2]), real_forward(x[1::2])
    out = [None] * (n // 2 + 1)
    out[0] = (even[0][0] + odd[0][0], None)
    out[n // 2] = (even[0][0] - odd[0][0], None)
    out[n // 4] = (even[n // 4][0], -odd[n // 4][0])
    for k in range(1, n // 4):
        tr, ti = twist(odd[k], -k, n)
        er, ei = even[k]
        out[k] = (er + tr, ei + ti)
        out[n // 2 - k] = (er - tr, ti - ei)
    return out


def real_inverse(x):
    n = 2 * (len(x) - 1)
    if n == 2:
        return [x[0][0] + x[1][0]]
    even, odd = [None] * (n // 4 + 1), [None] * (n // 4 + 1)
    even[0] = (x[0][0] + x[n // 2][0], None)
    odd[0] = (x[0][0] - x[n // 2][0], None)
    even[n // 4] = (2.0 * x[n // 4][0], None)
    odd[n // 4] = (-2.0 * x[n // 4][1], None)
    for k in range(1, n // 4):
        ar, ai = x[k]
        br, bi = x[n // 2 - k]
        even[k] = (ar + br, ai - bi)
        odd[k] = twist((ar - br, ai + bi), k, n)
    out = [None] * (n // 2)
    out[0::2], out[1::2] = real_inverse(even), real_inverse(odd)
    return out


def complex_transform(x, sign):
    n = len(x)
    if n == 1:
        return x
    even, odd = complex_transform(x[0::2], sign), complex_transform(x[1::2], sign)
    low, high = [], []
    for k in range(n // 2):
        tr, ti = twist(odd[k], sign * k, n)
        er, ei = even[k]
        low.append((er + tr, ei + ti))
        high.append((er - tr, ei - ti))
    return low + high


def times(a, b):
    return a[0] * b[0] - a[1] * b[1], a[0] * b[1] + a[1] * b[0]


def times_conj(a, b):
    return a[0] * b[0] + a[1] * b[1], a[1] * b[0] - a[0] * b[1]


SEND_A = 5 * CHUNKS
SEND_B = 3 * B * ROWS
SEND_C = B * ROWS


def pack_kernel(k_hbm, v_hbm, spec_hbm, out_ref, k_ref, v_ref, spec_ref, sems):
    copies = [
        pltpu.make_async_copy(source, target, sems.at[i])
        for i, (source, target) in enumerate(
            ((k_hbm, k_ref), (v_hbm, v_ref), (spec_hbm, spec_ref))
        )
    ]
    for copy in copies:
        copy.start()
    copies[0].wait()
    copies[1].wait()
    product = k_ref[...].astype(jnp.float32) * v_ref[...].astype(jnp.float32)
    for chunk in range(CHUNKS):
        cols = slice(chunk * LANES, (chunk + 1) * LANES)
        out_ref[pl.ds(chunk, N_FAR, stride=SEND_A), :] = product[:, cols]
    copies[2].wait()
    for part in range(4):
        for chunk in range(CHUNKS):
            cols = slice(chunk * LANES, (chunk + 1) * LANES)
            place = (1 + part) * CHUNKS + chunk
            out_ref[pl.ds(place, N_FAR, stride=SEND_A), :] = spec_ref[part, :, cols]


def coarse_kernel(in_ref, out_ref):
    for b in range(B):
        tokens = [in_ref[pl.ds((a * B + b) * SEND_A, CHUNKS), :] for a in range(A)]
        freqs = real_forward(tokens + [None] * A)
        items = [(freqs[0][0], freqs[A][0])] + freqs[1:A]
        for i in range(A):
            for part in range(2):
                target = i * SEND_B + b * ROWS + part * CHUNKS
                out_ref[pl.ds(target, CHUNKS), :] = items[i][part]
                for side, q in enumerate(item_freqs(i)):
                    parity, a = source_of(q)
                    source = (a * B + b) * SEND_A + (1 + 2 * parity + part) * CHUNKS
                    target = i * SEND_B + (B + side * B + b) * ROWS + part * CHUNKS
                    out_ref[pl.ds(target, CHUNKS), :] = in_ref[pl.ds(source, CHUNKS), :]


def upper_rows():
    return lax.broadcasted_iota(jnp.int32, (ROWS, LANES), 0) < CHUNKS


def swap_halves(value):
    return pltpu.roll(value, CHUNKS, 0)


def split(value):
    high = value.astype(jnp.bfloat16)
    return high, (value - high.astype(jnp.float32)).astype(jnp.bfloat16)


def dense(xh_ref, xl_ref, high_ref, low_ref):
    def dot(a, b):
        return jnp.dot(a[...], b[...], preferred_element_type=jnp.float32)

    return dot(xh_ref, high_ref) + (dot(xl_ref, high_ref) + dot(xh_ref, low_ref))


def filter_kernel(
    place_ref, in_ref, gain_hbm, turn_ref, high_ref, low_ref, out_ref,
    re_ref, im_ref, xh_ref, xl_ref, gain_ref, sem,
):
    gain_copy = pltpu.make_async_copy(gain_hbm, gain_ref, sem)
    gain_copy.start()
    channel, item = place_ref[0], place_ref[1]
    packed = item == 0
    upper = upper_rows()
    keep = jnp.logical_or(upper, packed)
    signs = jnp.where(upper, 1.0, -1.0) * jnp.where(packed, 0.0, 1.0)
    steps = turn_ref[D + A + item // 2, item % 2]

    def turned(d):
        return tuple(
            jnp.broadcast_to(steps[:, at : at + 1], (ROWS, LANES)) for at in (d, D + d)
        )

    slow = (turn_ref[D + item, 0], turn_ref[D + item, 1])
    values = [None] * D
    for w in range(N_NEAR):
        for b in range(B):
            d = digit(w, b)
            value = in_ref[pl.ds(w * SEND_B + b * ROWS, ROWS), :]
            other = swap_halves(value)
            pair = (jnp.where(keep, value, other), jnp.where(upper, other, value) * signs)
            values[d] = times(times(pair, slow), turned(d))
    for kd, value in enumerate(complex_transform(values, -1)):
        w, b = freq_place(kd)
        at = (b * N_NEAR + w) * ROWS
        re_ref[pl.ds(at, ROWS), :], im_ref[pl.ds(at, ROWS), :] = times(
            value, (turn_ref[kd, 0], turn_ref[kd, 1])
        )
    gain_copy.wait()
    lane = lax.broadcasted_iota(jnp.int32, gain_ref.shape, 1)
    gain = jnp.sum(jnp.where(lane == channel, gain_ref[...], 0.0))
    half_rows = 2 * D
    step = 2 * N_NEAR
    blocks = []
    for side in range(2):
        for b in range(0, B, 2):
            first = (side * B + b) * N_NEAR
            blocks.append(
                (
                    slice(first, first + step),
                    slice(half_rows + first, half_rows + first + step),
                    b * N_NEAR * ROWS + side * CHUNKS,
                    (B + side * B + b) * ROWS,
                )
            )
    for top, bottom, start, _ in blocks:
        for rows, ref in ((top, re_ref), (bottom, im_ref)):
            for chunk in range(CHUNKS):
                cols = slice(chunk * LANES, (chunk + 1) * LANES)
                high, low = split(ref[pl.ds(start + chunk, step, stride=ROWS), :])
                xh_ref[rows, cols] = high
                xl_ref[rows, cols] = low
    mixed = dense(xh_ref, xl_ref, high_ref, low_ref)
    for top, bottom, _, start in blocks:
        for chunk in range(CHUNKS):
            cols = slice(chunk * LANES, (chunk + 1) * LANES)
            sine_cols = slice(T + chunk * LANES, T + (chunk + 1) * LANES)
            value = (
                mixed[top, cols] + mixed[bottom, sine_cols],
                mixed[bottom, cols] - mixed[top, sine_cols],
            )
            response = [
                jnp.concatenate(
                    [
                        in_ref[pl.ds(start + b * ROWS + part * CHUNKS + chunk, N_NEAR, stride=SEND_B), :]
                        for b in range(2)
                    ],
                    axis=0,
                )
                for part in range(2)
            ]
            for rows, part in zip((top, bottom), times(value, (response[0] + gain, response[1]))):
                high, low = split(part)
                xh_ref[rows, cols] = high
                xl_ref[rows, cols] = low
    mixed = dense(xh_ref, xl_ref, high_ref, low_ref)
    for top, bottom, start, _ in blocks:
        for chunk in range(CHUNKS):
            cols = slice(chunk * LANES, (chunk + 1) * LANES)
            sine_cols = slice(T + chunk * LANES, T + (chunk + 1) * LANES)
            place = pl.ds(start + chunk, step, stride=ROWS)
            re_ref[place, :] = mixed[top, cols] - mixed[bottom, sine_cols]
            im_ref[place, :] = mixed[bottom, cols] + mixed[top, sine_cols]
    values = []
    for kd in range(D):
        w, b = freq_place(kd)
        at = (b * N_NEAR + w) * ROWS
        value = (re_ref[pl.ds(at, ROWS), :], im_ref[pl.ds(at, ROWS), :])
        values.append(times_conj(value, (turn_ref[kd, 0], turn_ref[kd, 1])))
    values = complex_transform(values, 1)
    scale = jnp.where(packed, 1.0 / FULL, 0.5 / FULL)
    for w in range(N_NEAR):
        for b in range(B):
            d = digit(w, b)
            re, im = times_conj(times_conj(values[d], slow), turned(d))
            summed = jnp.where(upper, re + swap_halves(re), swap_halves(im) - im)
            out_ref[pl.ds(w * SEND_C + b * ROWS, ROWS), :] = (
                jnp.where(packed, re, summed) * scale
            )


def uncoarse_kernel(in_ref, out_ref):
    for b in range(B):
        items = [
            tuple(
                in_ref[pl.ds(i * SEND_C + b * ROWS + part * CHUNKS, CHUNKS), :]
                for part in range(2)
            )
            for i in range(A)
        ]
        freqs = [(items[0][0], None)] + items[1:] + [(items[0][1], None)]
        for a, value in enumerate(real_inverse(freqs)):
            out_ref[pl.ds((a * B + b) * CHUNKS, CHUNKS), :] = value


def gate_kernel(in_ref, q_ref, out_ref):
    for chunk in range(CHUNKS):
        cols = slice(chunk * LANES, (chunk + 1) * LANES)
        gated = q_ref[:, cols].astype(jnp.float32) * in_ref[pl.ds(chunk, N_FAR, stride=CHUNKS), :]
        out_ref[:, cols] = gated.astype(jnp.bfloat16)


def split_table(table):
    high = table.astype(np.float32).astype(ml_dtypes.bfloat16)
    low = (table - high.astype(np.float64)).astype(np.float32).astype(ml_dtypes.bfloat16)
    return high, low


def tables():
    t = np.arange(T)
    angle = 2 * np.pi * (t[:, None] * t[None, :] % T) / T
    high, low = split_table(np.concatenate([np.cos(angle), np.sin(angle)], axis=1))

    def parts(steps, period):
        angles = 2 * np.pi * (steps % period) / period
        return np.stack([np.cos(angles), -np.sin(angles)], axis=-3).astype(np.float32)

    freqs = np.array([item_freqs(i) for i in range(A)])
    slow = parts(freqs[:, :, None] * t, FULL).reshape(A, 2, ROWS, LANES)
    step = 2 * np.pi * (freqs[:, None, :] * np.arange(D)[:, None] % (2 * A * D)) / (2 * A * D)
    step = np.concatenate([np.cos(step), -np.sin(step)], axis=1).transpose(0, 2, 1)
    step = np.repeat(step, CHUNKS, axis=1).astype(np.float32).reshape(A // 2, 2, ROWS, LANES)
    fast = parts(np.arange(D)[:, None, None] * t * np.ones((1, 2, 1), int), D * T)
    return np.concatenate([fast.reshape(D, 2, ROWS, LANES), slow, step]), high, low


VMEM = pl.BlockSpec(memory_space=pltpu.VMEM)
SMEM = pl.BlockSpec(memory_space=pltpu.SMEM)
HBM = pl.BlockSpec(memory_space=pltpu.HBM)


def in_hbm(x):
    return pltpu.with_memory_space_constraint(jnp.asarray(x), pltpu.HBM)


def call(kernel, shape, in_specs, dtype=jnp.float32, scratch=(), limit=VMEM_LIMIT):
    return pl.pallas_call(
        kernel,
        out_shape=jax.ShapeDtypeStruct(shape, dtype),
        in_specs=in_specs,
        out_specs=VMEM,
        scratch_shapes=list(scratch),
        compiler_params=pltpu.CompilerParams(vmem_limit_bytes=limit),
    )


def run_pack(k_proj, v_proj, spectrum):
    return call(
        pack_kernel,
        (N_FAR * SEND_A, LANES),
        [HBM] * 3,
        scratch=[
            pltpu.VMEM(k_proj.shape, k_proj.dtype),
            pltpu.VMEM(v_proj.shape, v_proj.dtype),
            pltpu.VMEM(spectrum.shape, spectrum.dtype),
            pltpu.SemaphoreType.DMA((3,)),
        ],
    )(*(in_hbm(x) for x in (k_proj, v_proj, spectrum)))


def run_coarse(value):
    return call(coarse_kernel, (N_NEAR * SEND_B, LANES), [VMEM])(value)


def run_filter(place, value, gain):
    turns, high, low = tables()
    return call(
        filter_kernel,
        (N_NEAR * SEND_C, LANES),
        [SMEM, VMEM, HBM] + [VMEM] * 3,
        scratch=[pltpu.VMEM((D * ROWS, LANES), jnp.float32)] * 2
        + [pltpu.VMEM((4 * D, T), jnp.bfloat16)] * 2
        + [pltpu.VMEM((1, gain.size), jnp.float32), pltpu.SemaphoreType.DMA],
    )(place, value, in_hbm(gain.reshape(1, -1)), turns, high, low)


def run_uncoarse(value):
    return call(uncoarse_kernel, (N_FAR * CHUNKS, LANES), [VMEM])(value)


def run_gate(value, q_proj):
    return call(gate_kernel, q_proj.shape, [VMEM] * 2, dtype=jnp.bfloat16)(value, q_proj)


def exchange(value, axes, count):
    tile = 8 if value.shape[0] // count % 8 == 0 else 4
    blocks = value.reshape(count, -1, tile, LANES)
    return lax.all_to_all(blocks, axes, 0, 0, tiled=True).reshape(-1, LANES)


def local(q_proj, k_proj, v_proj, skip_gain, spectrum):
    value = run_pack(k_proj, v_proj, spectrum.reshape(4, *k_proj.shape))
    value = exchange(value, FAR, N_FAR)
    value = run_coarse(value)
    value = exchange(value, NEAR, N_NEAR)
    place = jnp.stack([lax.axis_index(FAR), lax.axis_index(NEAR)]).astype(jnp.int32)
    value = run_filter(place, value, skip_gain)
    value = exchange(value, NEAR, N_NEAR)
    value = run_uncoarse(value)
    value = exchange(value, FAR, N_FAR)
    return run_gate(value, q_proj)


def solution(mesh):
    fine = Mesh(mesh.devices.reshape(SIZES), AXES)
    placed = (P(None, AXES), P(None, AXES), P(None, AXES), P(), P(None, None, None, AXES))
    return jax.shard_map(
        local, mesh=fine, in_specs=placed, out_specs=P(None, AXES), check_vma=False
    )
```

```python
import math

import jax
import jax.numpy as jnp
import ml_dtypes
import numpy as np
from jax import lax
from jax.experimental import pallas as pl
from jax.experimental.pallas import tpu as pltpu
from jax.sharding import Mesh, PartitionSpec as P

AXES = ("xl", "yh", "yl", "core", "xh", "zh", "zl")
SIZES = (2, 4, 2, 2, 2, 4, 2)
FAR = ("xl", "yh", "yl", "zh")
NEAR = ("core", "xh", "zl")
A = 8
B = 8
N_FAR = A * B
N_NEAR = 8
D = B * N_NEAR
T = 512
LANES = 128
CHUNKS = T // LANES
ROWS = 2 * CHUNKS
FULL = 2 * A * D * T
VMEM_LIMIT = 12 * 1024 * 1024


def item_freqs(i):
    return (0, 8) if i == 0 else (i, 16 - i)


def source_of(q):
    xl, y2, y1 = q >> 1 & 1, q >> 2 & 1, q >> 3 & 1
    return q & 1, xl * 4 + y2 * 2 + y1


def digit(w, b):
    core, xh, zl = w >> 2, w >> 1 & 1, w & 1
    yl, zh = b >> 2, b & 3
    return yl * 32 + core * 16 + xh * 8 + zh * 2 + zl


def freq_place(kd):
    y0, core, z0, z1, z2, xh = (kd >> bit & 1 for bit in range(6))
    return core * 4 + xh * 2 + z0, y0 * 4 + z2 * 2 + z1


def add(a, b):
    if a is None:
        return b
    return a if b is None else a + b


def sub(a, b):
    if b is None:
        return a
    return -b if a is None else a - b


def twist(value, steps, period):
    re, im = value
    eighth = 8 * steps % (8 * period)
    if eighth == 0:
        return value
    if eighth == 2 * period:
        return -im, re
    if eighth == 4 * period:
        return -re, -im
    if eighth == 6 * period:
        return im, -re
    c = math.cos(2 * math.pi * steps / period)
    s = math.sin(2 * math.pi * steps / period)
    if abs(abs(c) - abs(s)) < 1e-12:
        r = math.sqrt(0.5)
        cs, ss = math.copysign(1.0, c), math.copysign(1.0, s)
        a = re if cs > 0 else -re
        b = im if cs > 0 else -im
        return (
            ((a - im) if ss > 0 else (a + im)) * r,
            ((b + re) if ss > 0 else (b - re)) * r,
        )
    return re * c - im * s, re * s + im * c


def real_forward(x):
    n = len(x)
    if n == 2:
        return [(add(x[0], x[1]), None), (sub(x[0], x[1]), None)]
    even, odd = real_forward(x[0::2]), real_forward(x[1::2])
    out = [None] * (n // 2 + 1)
    out[0] = (even[0][0] + odd[0][0], None)
    out[n // 2] = (even[0][0] - odd[0][0], None)
    out[n // 4] = (even[n // 4][0], -odd[n // 4][0])
    for k in range(1, n // 4):
        tr, ti = twist(odd[k], -k, n)
        er, ei = even[k]
        out[k] = (er + tr, ei + ti)
        out[n // 2 - k] = (er - tr, ti - ei)
    return out


def real_inverse(x):
    n = 2 * (len(x) - 1)
    if n == 2:
        return [x[0][0] + x[1][0]]
    even, odd = [None] * (n // 4 + 1), [None] * (n // 4 + 1)
    even[0] = (x[0][0] + x[n // 2][0], None)
    odd[0] = (x[0][0] - x[n // 2][0], None)
    even[n // 4] = (2.0 * x[n // 4][0], None)
    odd[n // 4] = (-2.0 * x[n // 4][1], None)
    for k in range(1, n // 4):
        ar, ai = x[k]
        br, bi = x[n // 2 - k]
        even[k] = (ar + br, ai - bi)
        odd[k] = twist((ar - br, ai + bi), k, n)
    out = [None] * (n // 2)
    out[0::2], out[1::2] = real_inverse(even), real_inverse(odd)
    return out


def complex_transform(x, sign):
    n = len(x)
    if n == 1:
        return x
    even, odd = complex_transform(x[0::2], sign), complex_transform(x[1::2], sign)
    low, high = [], []
    for k in range(n // 2):
        tr, ti = twist(odd[k], sign * k, n)
        er, ei = even[k]
        low.append((er + tr, ei + ti))
        high.append((er - tr, ei - ti))
    return low + high


def times(a, b):
    return a[0] * b[0] - a[1] * b[1], a[0] * b[1] + a[1] * b[0]


def times_conj(a, b):
    return a[0] * b[0] + a[1] * b[1], a[1] * b[0] - a[0] * b[1]


SEND_A = 5 * CHUNKS
SEND_B = 3 * B * ROWS
SEND_C = B * ROWS


def pack_kernel(k_hbm, v_hbm, spec_hbm, out_ref, k_ref, v_ref, spec_ref, sems):
    copies = [
        pltpu.make_async_copy(source, target, sems.at[i])
        for i, (source, target) in enumerate(
            ((k_hbm, k_ref), (v_hbm, v_ref), (spec_hbm, spec_ref))
        )
    ]
    for copy in copies:
        copy.start()
    copies[0].wait()
    copies[1].wait()
    product = k_ref[...].astype(jnp.float32) * v_ref[...].astype(jnp.float32)
    for chunk in range(CHUNKS):
        cols = slice(chunk * LANES, (chunk + 1) * LANES)
        out_ref[pl.ds(chunk, N_FAR, stride=SEND_A), :] = product[:, cols]
    copies[2].wait()
    for part in range(4):
        for chunk in range(CHUNKS):
            cols = slice(chunk * LANES, (chunk + 1) * LANES)
            place = (1 + part) * CHUNKS + chunk
            out_ref[pl.ds(place, N_FAR, stride=SEND_A), :] = spec_ref[part, :, cols]


def coarse_kernel(in_ref, out_ref):
    for b in range(B):
        tokens = [in_ref[pl.ds((a * B + b) * SEND_A, CHUNKS), :] for a in range(A)]
        freqs = real_forward(tokens + [None] * A)
        items = [(freqs[0][0], freqs[A][0])] + freqs[1:A]
        for i in range(A):
            for part in range(2):
                target = i * SEND_B + b * ROWS + part * CHUNKS
                out_ref[pl.ds(target, CHUNKS), :] = items[i][part]
                for side, q in enumerate(item_freqs(i)):
                    parity, a = source_of(q)
                    source = (a * B + b) * SEND_A + (1 + 2 * parity + part) * CHUNKS
                    target = i * SEND_B + (B + side * B + b) * ROWS + part * CHUNKS
                    out_ref[pl.ds(target, CHUNKS), :] = in_ref[pl.ds(source, CHUNKS), :]


def upper_rows():
    return lax.broadcasted_iota(jnp.int32, (ROWS, LANES), 0) < CHUNKS


def swap_halves(value):
    return pltpu.roll(value, CHUNKS, 0)


def split(value):
    high = value.astype(jnp.bfloat16)
    return high, (value - high.astype(jnp.float32)).astype(jnp.bfloat16)


def dense(xh_ref, xl_ref, high_ref, low_ref):
    def dot(a, b):
        return jnp.dot(a[...], b[...], preferred_element_type=jnp.float32)

    return dot(xh_ref, high_ref) + (dot(xl_ref, high_ref) + dot(xh_ref, low_ref))


def filter_kernel(
    place_ref, in_ref, gain_hbm, turn_ref, high_ref, low_ref, out_ref,
    re_ref, im_ref, xh_ref, xl_ref, gain_ref, sem,
):
    gain_copy = pltpu.make_async_copy(gain_hbm, gain_ref, sem)
    gain_copy.start()
    channel, item = place_ref[0], place_ref[1]
    packed = item == 0
    upper = upper_rows()
    keep = jnp.logical_or(upper, packed)
    signs = jnp.where(upper, 1.0, -1.0) * jnp.where(packed, 0.0, 1.0)
    steps = turn_ref[D + A + item // 2, item % 2]

    def turned(d):
        return tuple(
            jnp.broadcast_to(steps[:, at : at + 1], (ROWS, LANES)) for at in (d, D + d)
        )

    slow = (turn_ref[D + item, 0], turn_ref[D + item, 1])
    values = [None] * D
    for w in range(N_NEAR):
        for b in range(B):
            d = digit(w, b)
            value = in_ref[pl.ds(w * SEND_B + b * ROWS, ROWS), :]
            other = swap_halves(value)
            pair = (jnp.where(keep, value, other), jnp.where(upper, other, value) * signs)
            values[d] = times(times(pair, slow), turned(d))
    for kd, value in enumerate(complex_transform(values, -1)):
        w, b = freq_place(kd)
        at = (b * N_NEAR + w) * ROWS
        re_ref[pl.ds(at, ROWS), :], im_ref[pl.ds(at, ROWS), :] = times(
            value, (turn_ref[kd, 0], turn_ref[kd, 1])
        )
    gain_copy.wait()
    lane = lax.broadcasted_iota(jnp.int32, gain_ref.shape, 1)
    gain = jnp.sum(jnp.where(lane == channel, gain_ref[...], 0.0))
    half_rows = 2 * D
    step = 2 * N_NEAR
    blocks = []
    for side in range(2):
        for b in range(0, B, 2):
            first = (side * B + b) * N_NEAR
            blocks.append(
                (
                    slice(first, first + step),
                    slice(half_rows + first, half_rows + first + step),
                    b * N_NEAR * ROWS + side * CHUNKS,
                    (B + side * B + b) * ROWS,
                )
            )
    for top, bottom, start, _ in blocks:
        for rows, ref in ((top, re_ref), (bottom, im_ref)):
            for chunk in range(CHUNKS):
                cols = slice(chunk * LANES, (chunk + 1) * LANES)
                high, low = split(ref[pl.ds(start + chunk, step, stride=ROWS), :])
                xh_ref[rows, cols] = high
                xl_ref[rows, cols] = low
    mixed = dense(xh_ref, xl_ref, high_ref, low_ref)
    for top, bottom, _, start in blocks:
        for chunk in range(CHUNKS):
            cols = slice(chunk * LANES, (chunk + 1) * LANES)
            sine_cols = slice(T + chunk * LANES, T + (chunk + 1) * LANES)
            value = (
                mixed[top, cols] + mixed[bottom, sine_cols],
                mixed[bottom, cols] - mixed[top, sine_cols],
            )
            response = [
                jnp.concatenate(
                    [
                        in_ref[pl.ds(start + b * ROWS + part * CHUNKS + chunk, N_NEAR, stride=SEND_B), :]
                        for b in range(2)
                    ],
                    axis=0,
                )
                for part in range(2)
            ]
            for rows, part in zip((top, bottom), times(value, (response[0] + gain, response[1]))):
                high, low = split(part)
                xh_ref[rows, cols] = high
                xl_ref[rows, cols] = low
    mixed = dense(xh_ref, xl_ref, high_ref, low_ref)
    for top, bottom, start, _ in blocks:
        for chunk in range(CHUNKS):
            cols = slice(chunk * LANES, (chunk + 1) * LANES)
            sine_cols = slice(T + chunk * LANES, T + (chunk + 1) * LANES)
            place = pl.ds(start + chunk, step, stride=ROWS)
            re_ref[place, :] = mixed[top, cols] - mixed[bottom, sine_cols]
            im_ref[place, :] = mixed[bottom, cols] + mixed[top, sine_cols]
    values = []
    for kd in range(D):
        w, b = freq_place(kd)
        at = (b * N_NEAR + w) * ROWS
        value = (re_ref[pl.ds(at, ROWS), :], im_ref[pl.ds(at, ROWS), :])
        values.append(times_conj(value, (turn_ref[kd, 0], turn_ref[kd, 1])))
    values = complex_transform(values, 1)
    scale = jnp.where(packed, 1.0 / FULL, 0.5 / FULL)
    for w in range(N_NEAR):
        for b in range(B):
            d = digit(w, b)
            re, im = times_conj(times_conj(values[d], slow), turned(d))
            summed = jnp.where(upper, re + swap_halves(re), swap_halves(im) - im)
            out_ref[pl.ds(w * SEND_C + b * ROWS, ROWS), :] = (
                jnp.where(packed, re, summed) * scale
            )


def uncoarse_kernel(in_ref, out_ref):
    for b in range(B):
        items = [
            tuple(
                in_ref[pl.ds(i * SEND_C + b * ROWS + part * CHUNKS, CHUNKS), :]
                for part in range(2)
            )
            for i in range(A)
        ]
        freqs = [(items[0][0], None)] + items[1:] + [(items[0][1], None)]
        for a, value in enumerate(real_inverse(freqs)):
            out_ref[pl.ds((a * B + b) * CHUNKS, CHUNKS), :] = value


def gate_kernel(in_ref, q_ref, out_ref):
    for chunk in range(CHUNKS):
        cols = slice(chunk * LANES, (chunk + 1) * LANES)
        gated = q_ref[:, cols].astype(jnp.float32) * in_ref[pl.ds(chunk, N_FAR, stride=CHUNKS), :]
        out_ref[:, cols] = gated.astype(jnp.bfloat16)


def split_table(table):
    high = table.astype(np.float32).astype(ml_dtypes.bfloat16)
    low = (table - high.astype(np.float64)).astype(np.float32).astype(ml_dtypes.bfloat16)
    return high, low


def tables():
    t = np.arange(T)
    angle = 2 * np.pi * (t[:, None] * t[None, :] % T) / T
    high, low = split_table(np.concatenate([np.cos(angle), np.sin(angle)], axis=1))

    def parts(steps, period):
        angles = 2 * np.pi * (steps % period) / period
        return np.stack([np.cos(angles), -np.sin(angles)], axis=-3).astype(np.float32)

    freqs = np.array([item_freqs(i) for i in range(A)])
    slow = parts(freqs[:, :, None] * t, FULL).reshape(A, 2, ROWS, LANES)
    step = 2 * np.pi * (freqs[:, None, :] * np.arange(D)[:, None] % (2 * A * D)) / (2 * A * D)
    step = np.concatenate([np.cos(step), -np.sin(step)], axis=1).transpose(0, 2, 1)
    step = np.repeat(step, CHUNKS, axis=1).astype(np.float32).reshape(A // 2, 2, ROWS, LANES)
    fast = parts(np.arange(D)[:, None, None] * t * np.ones((1, 2, 1), int), D * T)
    return np.concatenate([fast.reshape(D, 2, ROWS, LANES), slow, step]), high, low


VMEM = pl.BlockSpec(memory_space=pltpu.VMEM)
SMEM = pl.BlockSpec(memory_space=pltpu.SMEM)
HBM = pl.BlockSpec(memory_space=pltpu.HBM)


def in_hbm(x):
    return pltpu.with_memory_space_constraint(jnp.asarray(x), pltpu.HBM)


def call(kernel, shape, in_specs, dtype=jnp.float32, scratch=(), limit=VMEM_LIMIT):
    return pl.pallas_call(
        kernel,
        out_shape=jax.ShapeDtypeStruct(shape, dtype),
        in_specs=in_specs,
        out_specs=VMEM,
        scratch_shapes=list(scratch),
        compiler_params=pltpu.CompilerParams(vmem_limit_bytes=limit),
    )


def run_pack(k_proj, v_proj, spectrum):
    return call(
        pack_kernel,
        (N_FAR * SEND_A, LANES),
        [HBM] * 3,
        scratch=[
            pltpu.VMEM(k_proj.shape, k_proj.dtype),
            pltpu.VMEM(v_proj.shape, v_proj.dtype),
            pltpu.VMEM(spectrum.shape, spectrum.dtype),
            pltpu.SemaphoreType.DMA((3,)),
        ],
    )(*(in_hbm(x) for x in (k_proj, v_proj, spectrum)))


def run_coarse(value):
    return call(coarse_kernel, (N_NEAR * SEND_B, LANES), [VMEM])(value)


def run_filter(place, value, gain):
    turns, high, low = tables()
    return call(
        filter_kernel,
        (N_NEAR * SEND_C, LANES),
        [SMEM, VMEM, HBM] + [VMEM] * 3,
        scratch=[pltpu.VMEM((D * ROWS, LANES), jnp.float32)] * 2
        + [pltpu.VMEM((4 * D, T), jnp.bfloat16)] * 2
        + [pltpu.VMEM((1, gain.size), jnp.float32), pltpu.SemaphoreType.DMA],
    )(place, value, in_hbm(gain.reshape(1, -1)), turns, high, low)


def run_uncoarse(value):
    return call(uncoarse_kernel, (N_FAR * CHUNKS, LANES), [VMEM])(value)


def run_gate(value, q_proj):
    return call(gate_kernel, q_proj.shape, [VMEM] * 2, dtype=jnp.bfloat16)(value, q_proj)


def exchange(value, axes, count):
    tile = 8 if value.shape[0] // count % 8 == 0 else 4
    blocks = value.reshape(count, -1, tile, LANES)
    return lax.all_to_all(blocks, axes, 0, 0, tiled=True).reshape(-1, LANES)


def local(q_proj, k_proj, v_proj, skip_gain, spectrum):
    place = jnp.stack([lax.axis_index(FAR), lax.axis_index(NEAR)]).astype(jnp.int32)
    value = run_pack(k_proj, v_proj, spectrum.reshape(4, *k_proj.shape))
    value, place = lax.optimization_barrier((value, place))
    value = exchange(value, FAR, N_FAR)
    value = run_coarse(value)
    value = exchange(value, NEAR, N_NEAR)
    value = run_filter(place, value, skip_gain)
    value = exchange(value, NEAR, N_NEAR)
    value = run_uncoarse(value)
    value = exchange(value, FAR, N_FAR)
    return run_gate(value, q_proj)


def solution(mesh):
    fine = Mesh(mesh.devices.reshape(SIZES), AXES)
    placed = (P(None, AXES), P(None, AXES), P(None, AXES), P(), P(None, None, None, AXES))
    return jax.shard_map(
        local, mesh=fine, in_specs=placed, out_specs=P(None, AXES), check_vma=False
    )
```

```python
import math

import jax
import jax.numpy as jnp
import ml_dtypes
import numpy as np
from jax import lax
from jax.experimental import pallas as pl
from jax.experimental.pallas import tpu as pltpu
from jax.sharding import Mesh, PartitionSpec as P

AXES = ("xl", "yh", "yl", "core", "xh", "zh", "zl")
SIZES = (2, 4, 2, 2, 2, 4, 2)
FAR = ("xl", "yh", "zh", "zl")
NEAR = ("yl", "core", "xh")
A = 8
B = 8
N_FAR = A * B
N_NEAR = 8
D = B * N_NEAR
T = 512
LANES = 128
CHUNKS = T // LANES
ROWS = 2 * CHUNKS
FULL = 2 * A * D * T
VMEM_LIMIT = 24 * 1024 * 1024


def item_freqs(i):
    return (0, 8) if i == 0 else (i, 16 - i)


def source_of(q):
    xl, y2, y1 = q >> 1 & 1, q >> 2 & 1, q >> 3 & 1
    return q & 1, xl * 4 + y2 * 2 + y1


def digit(w, b):
    return w * 8 + b


def freq_place(kd):
    y0, core, z0, z1, z2, xh = (kd >> bit & 1 for bit in range(6))
    return y0 * 4 + core * 2 + xh, z2 * 4 + z1 * 2 + z0


def add(a, b):
    if a is None:
        return b
    return a if b is None else a + b


def sub(a, b):
    if b is None:
        return a
    return -b if a is None else a - b


def twist(value, steps, period):
    re, im = value
    eighth = 8 * steps % (8 * period)
    if eighth == 0:
        return value
    if eighth == 2 * period:
        return -im, re
    if eighth == 4 * period:
        return -re, -im
    if eighth == 6 * period:
        return im, -re
    c = math.cos(2 * math.pi * steps / period)
    s = math.sin(2 * math.pi * steps / period)
    if abs(abs(c) - abs(s)) < 1e-12:
        r = math.sqrt(0.5)
        cs, ss = math.copysign(1.0, c), math.copysign(1.0, s)
        a = re if cs > 0 else -re
        b = im if cs > 0 else -im
        return (
            ((a - im) if ss > 0 else (a + im)) * r,
            ((b + re) if ss > 0 else (b - re)) * r,
        )
    return re * c - im * s, re * s + im * c


def real_forward(x):
    n = len(x)
    if n == 2:
        return [(add(x[0], x[1]), None), (sub(x[0], x[1]), None)]
    even, odd = real_forward(x[0::2]), real_forward(x[1::2])
    out = [None] * (n // 2 + 1)
    out[0] = (even[0][0] + odd[0][0], None)
    out[n // 2] = (even[0][0] - odd[0][0], None)
    out[n // 4] = (even[n // 4][0], -odd[n // 4][0])
    for k in range(1, n // 4):
        tr, ti = twist(odd[k], -k, n)
        er, ei = even[k]
        out[k] = (er + tr, ei + ti)
        out[n // 2 - k] = (er - tr, ti - ei)
    return out


def real_inverse(x):
    n = 2 * (len(x) - 1)
    if n == 2:
        return [x[0][0] + x[1][0]]
    even, odd = [None] * (n // 4 + 1), [None] * (n // 4 + 1)
    even[0] = (x[0][0] + x[n // 2][0], None)
    odd[0] = (x[0][0] - x[n // 2][0], None)
    even[n // 4] = (2.0 * x[n // 4][0], None)
    odd[n // 4] = (-2.0 * x[n // 4][1], None)
    for k in range(1, n // 4):
        ar, ai = x[k]
        br, bi = x[n // 2 - k]
        even[k] = (ar + br, ai - bi)
        odd[k] = twist((ar - br, ai + bi), k, n)
    out = [None] * (n // 2)
    out[0::2], out[1::2] = real_inverse(even), real_inverse(odd)
    return out


def complex_transform(x, sign):
    n = len(x)
    if n == 1:
        return x
    even, odd = complex_transform(x[0::2], sign), complex_transform(x[1::2], sign)
    low, high = [], []
    for k in range(n // 2):
        tr, ti = twist(odd[k], sign * k, n)
        er, ei = even[k]
        low.append((er + tr, ei + ti))
        high.append((er - tr, ei - ti))
    return low + high


def times(a, b):
    return a[0] * b[0] - a[1] * b[1], a[0] * b[1] + a[1] * b[0]


def times_conj(a, b):
    return a[0] * b[0] + a[1] * b[1], a[1] * b[0] - a[0] * b[1]


SEND_A = 5 * CHUNKS
SEND_B = 3 * B * ROWS
SEND_C = B * ROWS
PITCH = (2 * B + 1) * ROWS


def pack_kernel(
    k_hbm, v_hbm, gain_hbm, spec_hbm, out_ref, k_ref, v_ref, gain_ref, spec_ref, sems
):
    copies = [
        pltpu.make_async_copy(source, target, sems.at[i])
        for i, (source, target) in enumerate(
            ((k_hbm, k_ref), (v_hbm, v_ref), (gain_hbm, gain_ref), (spec_hbm, spec_ref))
        )
    ]
    for copy in copies:
        copy.start()
    copies[0].wait()
    copies[1].wait()
    product = k_ref[...].astype(jnp.float32) * v_ref[...].astype(jnp.float32)
    for chunk in range(CHUNKS):
        cols = slice(chunk * LANES, (chunk + 1) * LANES)
        out_ref[pl.ds(chunk, N_FAR, stride=SEND_A), :] = product[:, cols]
    copies[2].wait()
    row = lax.broadcasted_iota(jnp.int32, (N_FAR, N_FAR), 0)
    col = lax.broadcasted_iota(jnp.int32, (N_FAR, N_FAR), 1)
    spread = jnp.broadcast_to(gain_ref[...], (N_FAR, N_FAR))
    gain = jnp.sum(jnp.where(row == col, spread, 0.0), axis=1, keepdims=True)
    copies[3].wait()
    for part in range(4):
        for chunk in range(CHUNKS):
            cols = slice(chunk * LANES, (chunk + 1) * LANES)
            place = (1 + part) * CHUNKS + chunk
            value = spec_ref[part, :, cols]
            value = value + gain if part % 2 == 0 else value
            out_ref[pl.ds(place, N_FAR, stride=SEND_A), :] = value


def coarse_kernel(in_ref, out_ref):
    for b in range(B):
        tokens = [in_ref[pl.ds((a * B + b) * SEND_A, CHUNKS), :] for a in range(A)]
        freqs = real_forward(tokens + [None] * A)
        items = [(freqs[0][0], freqs[A][0])] + freqs[1:A]
        for i in range(A):
            for part in range(2):
                target = i * SEND_B + b * ROWS + part * CHUNKS
                out_ref[pl.ds(target, CHUNKS), :] = items[i][part]
                for side, q in enumerate(item_freqs(i)):
                    parity, a = source_of(q)
                    source = (a * B + b) * SEND_A + (1 + 2 * parity + part) * CHUNKS
                    target = i * SEND_B + (B + side * B + b) * ROWS + part * CHUNKS
                    out_ref[pl.ds(target, CHUNKS), :] = in_ref[pl.ds(source, CHUNKS), :]


def upper_rows():
    return lax.broadcasted_iota(jnp.int32, (ROWS, LANES), 0) < CHUNKS


def swap_halves(value):
    return pltpu.roll(value, CHUNKS, 0)


def split(value):
    high = value.astype(jnp.bfloat16)
    return high, (value - high.astype(jnp.float32)).astype(jnp.bfloat16)


def dense(xh_ref, xl_ref, high_ref, low_ref):
    def dot(a, b):
        return jnp.dot(a[...], b[...], preferred_element_type=jnp.float32)

    return dot(xh_ref, high_ref) + (dot(xl_ref, high_ref) + dot(xh_ref, low_ref))


def filter_kernel(
    item_ref, in_ref, turn_ref, high_ref, low_ref, out_ref,
    re_ref, im_ref, xh_ref, xl_ref, response_ref,
):
    item = item_ref[0]
    packed = item == 0
    for w in range(N_NEAR):
        for at in range(2 * B):
            response_ref[pl.ds(w * PITCH + at * ROWS, ROWS), :] = in_ref[
                pl.ds(w * SEND_B + (B + at) * ROWS, ROWS), :
            ]
    upper = upper_rows()
    keep = jnp.logical_or(upper, packed)
    signs = jnp.where(upper, 1.0, -1.0) * jnp.where(packed, 0.0, 1.0)
    steps = turn_ref[D + A + item // 2, item % 2]

    def turned(d):
        return tuple(
            jnp.broadcast_to(steps[:, at : at + 1], (ROWS, LANES)) for at in (d, D + d)
        )

    slow = (turn_ref[D + item, 0], turn_ref[D + item, 1])
    values = [None] * D
    for w in range(N_NEAR):
        for b in range(B):
            d = digit(w, b)
            value = in_ref[pl.ds(w * SEND_B + b * ROWS, ROWS), :]
            other = swap_halves(value)
            pair = (jnp.where(keep, value, other), jnp.where(upper, other, value) * signs)
            values[d] = times(times(pair, slow), turned(d))
    for kd, value in enumerate(complex_transform(values, -1)):
        w, b = freq_place(kd)
        at = (b * N_NEAR + w) * ROWS
        re_ref[pl.ds(at, ROWS), :], im_ref[pl.ds(at, ROWS), :] = times(
            value, (turn_ref[kd, 0], turn_ref[kd, 1])
        )
    half_rows = 2 * D
    step = 2 * N_NEAR
    blocks = []
    for side in range(2):
        for b in range(0, B, 2):
            first = (side * B + b) * N_NEAR
            blocks.append(
                (
                    slice(first, first + step),
                    slice(half_rows + first, half_rows + first + step),
                    b * N_NEAR * ROWS + side * CHUNKS,
                    (side * B + b) * ROWS,
                )
            )
    for top, bottom, start, _ in blocks:
        for rows, ref in ((top, re_ref), (bottom, im_ref)):
            for chunk in range(CHUNKS):
                cols = slice(chunk * LANES, (chunk + 1) * LANES)
                high, low = split(ref[pl.ds(start + chunk, step, stride=ROWS), :])
                xh_ref[rows, cols] = high
                xl_ref[rows, cols] = low
    mixed = dense(xh_ref, xl_ref, high_ref, low_ref)
    for top, bottom, _, start in blocks:
        for chunk in range(CHUNKS):
            cols = slice(chunk * LANES, (chunk + 1) * LANES)
            sine_cols = slice(T + chunk * LANES, T + (chunk + 1) * LANES)
            value = (
                mixed[top, cols] + mixed[bottom, sine_cols],
                mixed[bottom, cols] - mixed[top, sine_cols],
            )
            response = [
                jnp.concatenate(
                    [
                        response_ref[pl.ds(start + b * ROWS + part * CHUNKS + chunk, N_NEAR, stride=PITCH), :]
                        for b in range(2)
                    ],
                    axis=0,
                )
                for part in range(2)
            ]
            for rows, part in zip((top, bottom), times(value, response)):
                high, low = split(part)
                xh_ref[rows, cols] = high
                xl_ref[rows, cols] = low
    mixed = dense(xh_ref, xl_ref, high_ref, low_ref)
    for top, bottom, start, _ in blocks:
        for chunk in range(CHUNKS):
            cols = slice(chunk * LANES, (chunk + 1) * LANES)
            sine_cols = slice(T + chunk * LANES, T + (chunk + 1) * LANES)
            place = pl.ds(start + chunk, step, stride=ROWS)
            re_ref[place, :] = mixed[top, cols] - mixed[bottom, sine_cols]
            im_ref[place, :] = mixed[bottom, cols] + mixed[top, sine_cols]
    values = []
    for kd in range(D):
        w, b = freq_place(kd)
        at = (b * N_NEAR + w) * ROWS
        value = (re_ref[pl.ds(at, ROWS), :], im_ref[pl.ds(at, ROWS), :])
        values.append(times_conj(value, (turn_ref[kd, 0], turn_ref[kd, 1])))
    values = complex_transform(values, 1)
    scale = jnp.where(packed, 1.0 / FULL, 0.5 / FULL)
    for w in range(N_NEAR):
        for b in range(B):
            d = digit(w, b)
            re, im = times_conj(times_conj(values[d], slow), turned(d))
            summed = jnp.where(upper, re + swap_halves(re), swap_halves(im) - im)
            out_ref[pl.ds(w * SEND_C + b * ROWS, ROWS), :] = (
                jnp.where(packed, re, summed) * scale
            )


def uncoarse_kernel(in_ref, out_ref):
    for b in range(B):
        items = [
            tuple(
                in_ref[pl.ds(i * SEND_C + b * ROWS + part * CHUNKS, CHUNKS), :]
                for part in range(2)
            )
            for i in range(A)
        ]
        freqs = [(items[0][0], None)] + items[1:] + [(items[0][1], None)]
        for a, value in enumerate(real_inverse(freqs)):
            out_ref[pl.ds((a * B + b) * CHUNKS, CHUNKS), :] = value


def gate_kernel(in_ref, q_ref, out_ref):
    for chunk in range(CHUNKS):
        cols = slice(chunk * LANES, (chunk + 1) * LANES)
        gated = q_ref[:, cols].astype(jnp.float32) * in_ref[pl.ds(chunk, N_FAR, stride=CHUNKS), :]
        out_ref[:, cols] = gated.astype(jnp.bfloat16)


def split_table(table):
    high = table.astype(np.float32).astype(ml_dtypes.bfloat16)
    low = (table - high.astype(np.float64)).astype(np.float32).astype(ml_dtypes.bfloat16)
    return high, low


def tables():
    t = np.arange(T)
    angle = 2 * np.pi * (t[:, None] * t[None, :] % T) / T
    high, low = split_table(np.concatenate([np.cos(angle), np.sin(angle)], axis=1))

    def parts(steps, period):
        angles = 2 * np.pi * (steps % period) / period
        return np.stack([np.cos(angles), -np.sin(angles)], axis=-3).astype(np.float32)

    freqs = np.array([item_freqs(i) for i in range(A)])
    slow = parts(freqs[:, :, None] * t, FULL).reshape(A, 2, ROWS, LANES)
    step = 2 * np.pi * (freqs[:, None, :] * np.arange(D)[:, None] % (2 * A * D)) / (2 * A * D)
    step = np.concatenate([np.cos(step), -np.sin(step)], axis=1).transpose(0, 2, 1)
    step = np.repeat(step, CHUNKS, axis=1).astype(np.float32).reshape(A // 2, 2, ROWS, LANES)
    fast = parts(np.arange(D)[:, None, None] * t * np.ones((1, 2, 1), int), D * T)
    return np.concatenate([fast.reshape(D, 2, ROWS, LANES), slow, step]), high, low


VMEM = pl.BlockSpec(memory_space=pltpu.VMEM)
SMEM = pl.BlockSpec(memory_space=pltpu.SMEM)
HBM = pl.BlockSpec(memory_space=pltpu.HBM)


def in_hbm(x):
    return pltpu.with_memory_space_constraint(jnp.asarray(x), pltpu.HBM)


def call(kernel, shape, in_specs, dtype=jnp.float32, scratch=(), limit=VMEM_LIMIT):
    return pl.pallas_call(
        kernel,
        out_shape=jax.ShapeDtypeStruct(shape, dtype),
        in_specs=in_specs,
        out_specs=VMEM,
        scratch_shapes=list(scratch),
        compiler_params=pltpu.CompilerParams(vmem_limit_bytes=limit),
    )


def run_pack(k_proj, v_proj, gain, spectrum):
    operands = (k_proj, v_proj, gain.reshape(1, -1), spectrum.reshape(4, *k_proj.shape))
    return call(
        pack_kernel,
        (N_FAR * SEND_A, LANES),
        [HBM] * 4,
        scratch=[pltpu.VMEM(x.shape, x.dtype) for x in operands]
        + [pltpu.SemaphoreType.DMA((4,))],
    )(*(in_hbm(x) for x in operands))


def run_coarse(value):
    return call(coarse_kernel, (N_NEAR * SEND_B, LANES), [VMEM])(value)


def run_filter(item, value):
    turns, high, low = tables()
    return call(
        filter_kernel,
        (N_NEAR * SEND_C, LANES),
        [SMEM] + [VMEM] * 4,
        scratch=[pltpu.VMEM((D * ROWS, LANES), jnp.float32)] * 2
        + [pltpu.VMEM((4 * D, T), jnp.bfloat16)] * 2
        + [
            pltpu.VMEM((N_NEAR * PITCH, LANES), jnp.float32),
        ],
    )(item, value, turns, high, low)


def run_uncoarse(value):
    return call(uncoarse_kernel, (N_FAR * CHUNKS, LANES), [VMEM])(value)


def run_gate(value, q_proj):
    return call(gate_kernel, q_proj.shape, [VMEM] * 2, dtype=jnp.bfloat16)(value, q_proj)


def exchange(value, axes, count):
    tile = 8 if value.shape[0] // count % 8 == 0 else 4
    blocks = value.reshape(count, -1, tile, LANES)
    return lax.all_to_all(blocks, axes, 0, 0, tiled=True).reshape(-1, LANES)


def local(q_proj, k_proj, v_proj, skip_gain, spectrum):
    item = lax.axis_index(NEAR).astype(jnp.int32).reshape(1)
    value = run_pack(k_proj, v_proj, skip_gain, spectrum)
    value, item = lax.optimization_barrier((value, item))
    value = exchange(value, FAR, N_FAR)
    value = run_coarse(value)
    value = exchange(value, NEAR, N_NEAR)
    value = run_filter(item, value)
    value = exchange(value, NEAR, N_NEAR)
    value = run_uncoarse(value)
    value = exchange(value, FAR, N_FAR)
    return run_gate(value, q_proj)


def solution(mesh):
    fine = Mesh(mesh.devices.reshape(SIZES), AXES)
    placed = (P(None, AXES), P(None, AXES), P(None, AXES), P(), P(None, None, None, AXES))
    return jax.shard_map(
        local, mesh=fine, in_specs=placed, out_specs=P(None, AXES), check_vma=False
    )
```

```python
import math

import jax
import jax.numpy as jnp
import ml_dtypes
import numpy as np
from jax import lax
from jax.experimental import pallas as pl
from jax.experimental.pallas import tpu as pltpu
from jax.sharding import Mesh, PartitionSpec as P

AXES = ("xl", "yh", "yl", "core", "xh", "zh", "zl")
SIZES = (2, 4, 2, 2, 2, 4, 2)
FAR = ("xl", "yh", "zh", "zl")
NEAR = ("yl", "core", "xh")
A = 8
B = 8
N_FAR = A * B
N_NEAR = 8
D = B * N_NEAR
T = 512
LANES = 128
CHUNKS = T // LANES
ROWS = 2 * CHUNKS
FULL = 2 * A * D * T
VMEM_LIMIT = 24 * 1024 * 1024


def item_freqs(i):
    return (0, 8) if i == 0 else (i, 16 - i)


def source_of(q):
    xl, y2, y1 = q >> 1 & 1, q >> 2 & 1, q >> 3 & 1
    return q & 1, xl * 4 + y2 * 2 + y1


def digit(w, b):
    return w * 8 + b


def freq_place(kd):
    y0, core, z0, z1, z2, xh = (kd >> bit & 1 for bit in range(6))
    return y0 * 4 + core * 2 + xh, z2 * 4 + z1 * 2 + z0


def add(a, b):
    if a is None:
        return b
    return a if b is None else a + b


def sub(a, b):
    if b is None:
        return a
    return -b if a is None else a - b


def twist(value, steps, period):
    re, im = value
    eighth = 8 * steps % (8 * period)
    if eighth == 0:
        return value
    if eighth == 2 * period:
        return -im, re
    if eighth == 4 * period:
        return -re, -im
    if eighth == 6 * period:
        return im, -re
    c = math.cos(2 * math.pi * steps / period)
    s = math.sin(2 * math.pi * steps / period)
    if abs(abs(c) - abs(s)) < 1e-12:
        r = math.sqrt(0.5)
        cs, ss = math.copysign(1.0, c), math.copysign(1.0, s)
        a = re if cs > 0 else -re
        b = im if cs > 0 else -im
        return (
            ((a - im) if ss > 0 else (a + im)) * r,
            ((b + re) if ss > 0 else (b - re)) * r,
        )
    return re * c - im * s, re * s + im * c


def real_forward(x):
    n = len(x)
    if n == 2:
        return [(add(x[0], x[1]), None), (sub(x[0], x[1]), None)]
    even, odd = real_forward(x[0::2]), real_forward(x[1::2])
    out = [None] * (n // 2 + 1)
    out[0] = (even[0][0] + odd[0][0], None)
    out[n // 2] = (even[0][0] - odd[0][0], None)
    out[n // 4] = (even[n // 4][0], -odd[n // 4][0])
    for k in range(1, n // 4):
        tr, ti = twist(odd[k], -k, n)
        er, ei = even[k]
        out[k] = (er + tr, ei + ti)
        out[n // 2 - k] = (er - tr, ti - ei)
    return out


def real_inverse(x):
    n = 2 * (len(x) - 1)
    if n == 2:
        return [x[0][0] + x[1][0]]
    even, odd = [None] * (n // 4 + 1), [None] * (n // 4 + 1)
    even[0] = (x[0][0] + x[n // 2][0], None)
    odd[0] = (x[0][0] - x[n // 2][0], None)
    even[n // 4] = (2.0 * x[n // 4][0], None)
    odd[n // 4] = (-2.0 * x[n // 4][1], None)
    for k in range(1, n // 4):
        ar, ai = x[k]
        br, bi = x[n // 2 - k]
        even[k] = (ar + br, ai - bi)
        odd[k] = twist((ar - br, ai + bi), k, n)
    out = [None] * (n // 2)
    out[0::2], out[1::2] = real_inverse(even), real_inverse(odd)
    return out


def complex_transform(x, sign):
    n = len(x)
    if n == 1:
        return x
    even, odd = complex_transform(x[0::2], sign), complex_transform(x[1::2], sign)
    low, high = [], []
    for k in range(n // 2):
        tr, ti = twist(odd[k], sign * k, n)
        er, ei = even[k]
        low.append((er + tr, ei + ti))
        high.append((er - tr, ei - ti))
    return low + high


def times(a, b):
    return a[0] * b[0] - a[1] * b[1], a[0] * b[1] + a[1] * b[0]


def times_conj(a, b):
    return a[0] * b[0] + a[1] * b[1], a[1] * b[0] - a[0] * b[1]


SEND_A = 5 * CHUNKS
SEND_B = 3 * B * ROWS
SEND_C = B * ROWS
PITCH = (2 * B + 1) * ROWS


def pack_kernel(
    k_hbm, v_hbm, gain_hbm, spec_hbm, out_ref, k_ref, v_ref, gain_ref, spec_ref, sems
):
    copies = [
        pltpu.make_async_copy(source, target, sems.at[i])
        for i, (source, target) in enumerate(
            ((k_hbm, k_ref), (v_hbm, v_ref), (gain_hbm, gain_ref), (spec_hbm, spec_ref))
        )
    ]
    for copy in copies:
        copy.start()
    copies[0].wait()
    copies[1].wait()
    product = k_ref[...].astype(jnp.float32) * v_ref[...].astype(jnp.float32)
    for chunk in range(CHUNKS):
        cols = slice(chunk * LANES, (chunk + 1) * LANES)
        out_ref[pl.ds(chunk, N_FAR, stride=SEND_A), :] = product[:, cols]
    copies[2].wait()
    row = lax.broadcasted_iota(jnp.int32, (N_FAR, N_FAR), 0)
    col = lax.broadcasted_iota(jnp.int32, (N_FAR, N_FAR), 1)
    spread = jnp.broadcast_to(gain_ref[...], (N_FAR, N_FAR))
    gain = jnp.sum(jnp.where(row == col, spread, 0.0), axis=1, keepdims=True)
    copies[3].wait()
    for part in range(4):
        for chunk in range(CHUNKS):
            cols = slice(chunk * LANES, (chunk + 1) * LANES)
            place = (1 + part) * CHUNKS + chunk
            value = spec_ref[part, :, cols]
            value = value + gain if part % 2 == 0 else value
            out_ref[pl.ds(place, N_FAR, stride=SEND_A), :] = value


def coarse_kernel(in_ref, out_ref):
    for b in range(B):
        tokens = [in_ref[pl.ds((a * B + b) * SEND_A, CHUNKS), :] for a in range(A)]
        freqs = real_forward(tokens + [None] * A)
        items = [(freqs[0][0], freqs[A][0])] + freqs[1:A]
        for i in range(A):
            for part in range(2):
                target = i * SEND_B + b * ROWS + part * CHUNKS
                out_ref[pl.ds(target, CHUNKS), :] = items[i][part]
                for side, q in enumerate(item_freqs(i)):
                    parity, a = source_of(q)
                    source = (a * B + b) * SEND_A + (1 + 2 * parity + part) * CHUNKS
                    target = i * SEND_B + (B + side * B + b) * ROWS + part * CHUNKS
                    out_ref[pl.ds(target, CHUNKS), :] = in_ref[pl.ds(source, CHUNKS), :]


def upper_rows():
    return lax.broadcasted_iota(jnp.int32, (ROWS, LANES), 0) < CHUNKS


def swap_halves(value):
    return pltpu.roll(value, CHUNKS, 0)


def split(value):
    high = value.astype(jnp.bfloat16)
    return high, (value - high.astype(jnp.float32)).astype(jnp.bfloat16)


def dense(x_ref, high_ref, low_ref):
    def dot(a, b):
        return jnp.dot(a, b[...], preferred_element_type=jnp.float32)

    both = dot(x_ref[...], high_ref)
    return both[: 4 * D] + (both[4 * D :] + dot(x_ref[: 4 * D, :], low_ref))


def filter_kernel(
    item_ref, in_ref, turn_ref, high_ref, low_ref, out_ref,
    re_ref, im_ref, x_ref, response_ref,
):
    item = item_ref[0]
    packed = item == 0
    for w in range(N_NEAR):
        for at in range(2 * B):
            response_ref[pl.ds(w * PITCH + at * ROWS, ROWS), :] = in_ref[
                pl.ds(w * SEND_B + (B + at) * ROWS, ROWS), :
            ]
    upper = upper_rows()
    keep = jnp.logical_or(upper, packed)
    signs = jnp.where(upper, 1.0, -1.0) * jnp.where(packed, 0.0, 1.0)
    steps = turn_ref[D + A + item // 2, item % 2]

    def turned(d):
        return tuple(
            jnp.broadcast_to(steps[:, at : at + 1], (ROWS, LANES)) for at in (d, D + d)
        )

    slow = (turn_ref[D + item, 0], turn_ref[D + item, 1])
    values = [None] * D
    for w in range(N_NEAR):
        for b in range(B):
            d = digit(w, b)
            value = in_ref[pl.ds(w * SEND_B + b * ROWS, ROWS), :]
            other = swap_halves(value)
            pair = (jnp.where(keep, value, other), jnp.where(upper, other, value) * signs)
            values[d] = times(times(pair, slow), turned(d))
    for kd, value in enumerate(complex_transform(values, -1)):
        w, b = freq_place(kd)
        at = (b * N_NEAR + w) * ROWS
        re_ref[pl.ds(at, ROWS), :], im_ref[pl.ds(at, ROWS), :] = times(
            value, (turn_ref[kd, 0], turn_ref[kd, 1])
        )
    half_rows = 2 * D
    step = 2 * N_NEAR
    blocks = []
    for side in range(2):
        for b in range(0, B, 2):
            first = (side * B + b) * N_NEAR
            blocks.append(
                (
                    slice(first, first + step),
                    slice(half_rows + first, half_rows + first + step),
                    b * N_NEAR * ROWS + side * CHUNKS,
                    (side * B + b) * ROWS,
                )
            )
    for top, bottom, start, _ in blocks:
        for rows, ref in ((top, re_ref), (bottom, im_ref)):
            for chunk in range(CHUNKS):
                cols = slice(chunk * LANES, (chunk + 1) * LANES)
                high, low = split(ref[pl.ds(start + chunk, step, stride=ROWS), :])
                x_ref[rows, cols] = high
                x_ref[slice(rows.start + 4 * D, rows.stop + 4 * D), cols] = low
    mixed = dense(x_ref, high_ref, low_ref)
    for top, bottom, _, start in blocks:
        for chunk in range(CHUNKS):
            cols = slice(chunk * LANES, (chunk + 1) * LANES)
            sine_cols = slice(T + chunk * LANES, T + (chunk + 1) * LANES)
            value = (
                mixed[top, cols] + mixed[bottom, sine_cols],
                mixed[bottom, cols] - mixed[top, sine_cols],
            )
            response = [
                jnp.concatenate(
                    [
                        response_ref[pl.ds(start + b * ROWS + part * CHUNKS + chunk, N_NEAR, stride=PITCH), :]
                        for b in range(2)
                    ],
                    axis=0,
                )
                for part in range(2)
            ]
            for rows, part in zip((top, bottom), times(value, response)):
                high, low = split(part)
                x_ref[rows, cols] = high
                x_ref[slice(rows.start + 4 * D, rows.stop + 4 * D), cols] = low
    mixed = dense(x_ref, high_ref, low_ref)
    for top, bottom, start, _ in blocks:
        for chunk in range(CHUNKS):
            cols = slice(chunk * LANES, (chunk + 1) * LANES)
            sine_cols = slice(T + chunk * LANES, T + (chunk + 1) * LANES)
            place = pl.ds(start + chunk, step, stride=ROWS)
            re_ref[place, :] = mixed[top, cols] - mixed[bottom, sine_cols]
            im_ref[place, :] = mixed[bottom, cols] + mixed[top, sine_cols]
    values = []
    for kd in range(D):
        w, b = freq_place(kd)
        at = (b * N_NEAR + w) * ROWS
        value = (re_ref[pl.ds(at, ROWS), :], im_ref[pl.ds(at, ROWS), :])
        values.append(times_conj(value, (turn_ref[kd, 0], turn_ref[kd, 1])))
    values = complex_transform(values, 1)
    scale = jnp.where(packed, 1.0 / FULL, 0.5 / FULL)
    for w in range(N_NEAR):
        for b in range(B):
            d = digit(w, b)
            re, im = times_conj(times_conj(values[d], slow), turned(d))
            summed = jnp.where(upper, re + swap_halves(re), swap_halves(im) - im)
            out_ref[pl.ds(w * SEND_C + b * ROWS, ROWS), :] = (
                jnp.where(packed, re, summed) * scale
            )


def uncoarse_kernel(in_ref, out_ref):
    for b in range(B):
        items = [
            tuple(
                in_ref[pl.ds(i * SEND_C + b * ROWS + part * CHUNKS, CHUNKS), :]
                for part in range(2)
            )
            for i in range(A)
        ]
        freqs = [(items[0][0], None)] + items[1:] + [(items[0][1], None)]
        for a, value in enumerate(real_inverse(freqs)):
            out_ref[pl.ds((a * B + b) * CHUNKS, CHUNKS), :] = value


def gate_kernel(in_ref, q_ref, out_ref):
    for chunk in range(CHUNKS):
        cols = slice(chunk * LANES, (chunk + 1) * LANES)
        gated = q_ref[:, cols].astype(jnp.float32) * in_ref[pl.ds(chunk, N_FAR, stride=CHUNKS), :]
        out_ref[:, cols] = gated.astype(jnp.bfloat16)


def split_table(table):
    high = table.astype(np.float32).astype(ml_dtypes.bfloat16)
    low = (table - high.astype(np.float64)).astype(np.float32).astype(ml_dtypes.bfloat16)
    return high, low


def tables():
    t = np.arange(T)
    angle = 2 * np.pi * (t[:, None] * t[None, :] % T) / T
    high, low = split_table(np.concatenate([np.cos(angle), np.sin(angle)], axis=1))

    def parts(steps, period):
        angles = 2 * np.pi * (steps % period) / period
        return np.stack([np.cos(angles), -np.sin(angles)], axis=-3).astype(np.float32)

    freqs = np.array([item_freqs(i) for i in range(A)])
    slow = parts(freqs[:, :, None] * t, FULL).reshape(A, 2, ROWS, LANES)
    step = 2 * np.pi * (freqs[:, None, :] * np.arange(D)[:, None] % (2 * A * D)) / (2 * A * D)
    step = np.concatenate([np.cos(step), -np.sin(step)], axis=1).transpose(0, 2, 1)
    step = np.repeat(step, CHUNKS, axis=1).astype(np.float32).reshape(A // 2, 2, ROWS, LANES)
    fast = parts(np.arange(D)[:, None, None] * t * np.ones((1, 2, 1), int), D * T)
    return np.concatenate([fast.reshape(D, 2, ROWS, LANES), slow, step]), high, low


VMEM = pl.BlockSpec(memory_space=pltpu.VMEM)
SMEM = pl.BlockSpec(memory_space=pltpu.SMEM)
HBM = pl.BlockSpec(memory_space=pltpu.HBM)


def in_hbm(x):
    return pltpu.with_memory_space_constraint(jnp.asarray(x), pltpu.HBM)


def call(kernel, shape, in_specs, dtype=jnp.float32, scratch=(), limit=VMEM_LIMIT):
    return pl.pallas_call(
        kernel,
        out_shape=jax.ShapeDtypeStruct(shape, dtype),
        in_specs=in_specs,
        out_specs=VMEM,
        scratch_shapes=list(scratch),
        compiler_params=pltpu.CompilerParams(vmem_limit_bytes=limit),
    )


def run_pack(k_proj, v_proj, gain, spectrum):
    operands = (k_proj, v_proj, gain.reshape(1, -1), spectrum.reshape(4, *k_proj.shape))
    return call(
        pack_kernel,
        (N_FAR * SEND_A, LANES),
        [HBM] * 4,
        scratch=[pltpu.VMEM(x.shape, x.dtype) for x in operands]
        + [pltpu.SemaphoreType.DMA((4,))],
    )(*(in_hbm(x) for x in operands))


def run_coarse(value):
    return call(coarse_kernel, (N_NEAR * SEND_B, LANES), [VMEM])(value)


def run_filter(item, value):
    turns, high, low = tables()
    return call(
        filter_kernel,
        (N_NEAR * SEND_C, LANES),
        [SMEM] + [VMEM] * 4,
        scratch=[pltpu.VMEM((D * ROWS, LANES), jnp.float32)] * 2
        + [
            pltpu.VMEM((8 * D, T), jnp.bfloat16),
            pltpu.VMEM((N_NEAR * PITCH, LANES), jnp.float32),
        ],
    )(item, value, turns, high, low)


def run_uncoarse(value):
    return call(uncoarse_kernel, (N_FAR * CHUNKS, LANES), [VMEM])(value)


def run_gate(value, q_proj):
    return call(gate_kernel, q_proj.shape, [VMEM] * 2, dtype=jnp.bfloat16)(value, q_proj)


def exchange(value, axes, count):
    tile = 8 if value.shape[0] // count % 8 == 0 else 4
    blocks = value.reshape(count, -1, tile, LANES)
    return lax.all_to_all(blocks, axes, 0, 0, tiled=True).reshape(-1, LANES)


def local(q_proj, k_proj, v_proj, skip_gain, spectrum):
    item = lax.axis_index(NEAR).astype(jnp.int32).reshape(1)
    value = run_pack(k_proj, v_proj, skip_gain, spectrum)
    value, item = lax.optimization_barrier((value, item))
    value = exchange(value, FAR, N_FAR)
    value = run_coarse(value)
    value = exchange(value, NEAR, N_NEAR)
    value = run_filter(item, value)
    value = exchange(value, NEAR, N_NEAR)
    value = run_uncoarse(value)
    value = exchange(value, FAR, N_FAR)
    return run_gate(value, q_proj)


def solution(mesh):
    fine = Mesh(mesh.devices.reshape(SIZES), AXES)
    placed = (P(None, AXES), P(None, AXES), P(None, AXES), P(), P(None, None, None, AXES))
    return jax.shard_map(
        local, mesh=fine, in_specs=placed, out_specs=P(None, AXES), check_vma=False
    )
```
